256 devices in a mesh: circ: 32 (over x_hi, z, core), radial: 4 (over y), side: 2 (over x_lo).
Axes of the slice: x: 4 (x_hi: 2, x_lo: 2; x = x_hi * 2 + x_lo), y: 4, z: 8, core: 2. Of those that a mesh axis runs over, the one named last changes fastest.
Arguments:
- current: float32 [2, 32, 4, 5, 216, 256], P('side', 'circ', 'radial'), may hold values from -6 to 6
- section_base: float32 [2, 32, 4, 5, 216, 256], P('side', 'circ', 'radial'), may hold values from -6 to 6
- metric: float32 [2, 32, 4, 3, 256], P('side', 'circ', 'radial'), may hold values from 0.5 to 2
- slot_cell: int32 [2, 32, 4, 256], P('side', 'circ', 'radial'), may hold values from 0 to 255, each once within a row
- rotation: int32 [1], replicated, may hold values from 0 to 255
- mortar_index: int32 [16], P('radial'), may hold values from 0 to 7
Outputs:
- advanced: float32 [2, 32, 4, 5, 216, 256], P('side', 'circ', 'radial')
The draws below stay inside these ranges and needn't reach their ends.
Inputs may be any that keep to these rules, and one draw needn't show every extreme that they name: `slot_cell`: each device's 256 slots hold each of its cells exactly once.
All inputs are finite; a program needn't handle non-finite values.
Results may differ from the reference program's by a relative error of at most 0.0001.
Values sent between devices are 32-bit elements; how exact they have to be, the bound alone decides.
No kernel may reach another device: no remote copies, remote signals or barrier semaphores. Data moves between devices by JAX's collectives and lax.ppermute only.
A program may use at most 128 MiB of HBM per device.

```python
import math
import jax
import jax.numpy as jnp
import numpy as np
from jax import lax

EL_C = 8
EL_R = 4
EL_A = 8
FRACS = 8
SECTORS = 32
BLOCKS = 4
ELEMS = 256


def with_ends(values, rng, smallest, high):
    place = [jax.random.randint(jax.random.fold_in(rng, axis), (), 0, length) for axis, length in enumerate(values.shape)]
    longest = values.shape.index(max(values.shape))
    neighbour = place[:longest] + [(place[longest] + 1) % values.shape[longest]] + place[longest + 1:]
    return values.at[tuple(place)].set(smallest).at[tuple(neighbour)].set(high)


def steps_of(own_key, dims, pieces, smallest, top_value):
    factor_of = 1.0
    for position, blocks in pieces:
        steps = jax.random.uniform(jax.random.fold_in(jax.random.fold_in(own_key, 6), position), (blocks,), jnp.float32, smallest / len(pieces), top_value / len(pieces))
        factor_of = factor_of * jnp.repeat(jnp.exp(steps), dims[position] // blocks).reshape((-1,) + (1,) * (len(dims) - 1 - position))
    return factor_of


def gaussian(stream_key, extent, scale, bound, split=(), kind=jnp.bfloat16):
    entries = jax.random.normal(stream_key, extent, jnp.float32) * scale
    if len(split) > 0:
        entries = steps_of(stream_key, extent, split, -0.22, 0.18) * entries
    return jnp.clip(entries, min=-bound, max=bound).astype(kind)


def setup_inputs(seed: int = 0) -> dict:
    keys = jax.random.split(jax.random.key(seed), 7)
    return {
        "current": gaussian(keys[0], (2, SECTORS, BLOCKS, 5, 216, ELEMS), 1.0, 6.0, ((0, 2), (1, 32), (2, 4)), jnp.float32),
        "section_base": gaussian(keys[1], (2, SECTORS, BLOCKS, 5, 216, ELEMS), 1.0, 6.0, ((0, 2), (1, 32), (2, 4)), jnp.float32),
        "metric": jnp.clip(jnp.exp(math.log(2.0) - 1.3862944 * jax.random.uniform(keys[2], (2, SECTORS, BLOCKS, 3, ELEMS), jnp.float32) ** steps_of(keys[2], (2, SECTORS, BLOCKS, 3, ELEMS), ((0, 2), (1, 32), (2, 4)), -0.2, 0.2)), 0.5, 2.0),
        "slot_cell": jax.vmap(lambda own: jax.random.permutation(own, ELEMS))(jax.random.split(keys[3], 2 * SECTORS * BLOCKS)).reshape((2, SECTORS, BLOCKS, ELEMS)).astype(jnp.int32),
        "rotation": jax.random.randint(keys[4], (1,), 0, EL_C * SECTORS).astype(jnp.int32),
        "mortar_index": with_ends(jax.random.randint(keys[5], (BLOCKS * EL_R,), 0, FRACS), jax.random.fold_in(keys[5], 1), 0, FRACS - 1).astype(jnp.int32),
    }


HIGH = lax.Precision.HIGHEST
FLOW = (0.3, -0.2, 0.25)
STEP = 0.02
END_WEIGHT = 1.0 / 15.0

def node_table():
    inner_point = math.sqrt(1.0 / 3.0 - 2.0 * math.sqrt(7.0) / 21.0)
    outer_point = math.sqrt(1.0 / 3.0 + 2.0 * math.sqrt(7.0) / 21.0)
    return np.array([-1.0, -outer_point, -inner_point, inner_point, outer_point, 1.0])

def derivative_table():
    abscissa = node_table()
    weights_bary = np.array([np.prod([abscissa[i] - abscissa[m] for m in range(6) if m != i]) for i in range(6)])
    matrix = np.zeros((6, 6))
    for i in range(6):
        for j in range(6):
            if i != j:
                matrix[i, j] = weights_bary[i] / (weights_bary[j] * (abscissa[i] - abscissa[j]))
        matrix[i, i] = -np.sum(matrix[i])
    return matrix

def basis_values(points):
    nodes_unit = (node_table() + 1.0) / 2.0
    values = np.ones((points.shape[0], 6))
    for j in range(6):
        for m in range(6):
            if m != j:
                values[:, j] = values[:, j] * (points - nodes_unit[m]) / (nodes_unit[j] - nodes_unit[m])
    return values

def mortar_tables():
    nodes_unit = (node_table() + 1.0) / 2.0
    tables = np.zeros((4, FRACS, 6, 6))
    for k in range(FRACS):
        fraction = k / FRACS
        beyond = nodes_unit >= fraction
        tables[0, k] = np.where(beyond[:, None], basis_values(nodes_unit - fraction), 0.0)
        tables[1, k] = np.where(beyond[:, None], 0.0, basis_values(nodes_unit - fraction + 1.0))
        crossing = nodes_unit + fraction >= 1.0
        tables[2, k] = np.where(crossing[:, None], 0.0, basis_values(nodes_unit + fraction))
        tables[3, k] = np.where(crossing[:, None], basis_values(nodes_unit + fraction - 1.0), 0.0)
    return tables

def flux_along(fields, direction):
    result = FLOW[direction] * fields
    result = result.at[0].add(fields[1 + direction])
    result = result.at[1 + direction].add(fields[0])
    return result

def mix_columns(matrices, traces):
    return jnp.einsum('rij,fjbcr->fibcr', matrices, traces, precision=HIGH)

def time_rate(field_grid, metric_grid, derivative, exterior):
    tendency = jnp.zeros_like(field_grid)
    for direction in range(3):
        node_axis = 1 + direction
        elem_axis = 3 + direction
        fluxes = flux_along(field_grid, direction)
        gradient = jnp.moveaxis(jnp.tensordot(derivative, fluxes, axes=((1,), (node_axis,)), precision=HIGH), 0, node_axis)
        tendency = tendency - metric_grid[direction] * gradient
        low_trace = jnp.take(field_grid, 0, axis=node_axis)
        high_trace = jnp.take(field_grid, 5, axis=node_axis)
        length = field_grid.shape[4 + direction]
        lower_side, upper_side = exterior[direction]
        low_outer = jnp.concatenate([jnp.expand_dims(lower_side, elem_axis), lax.slice_in_dim(high_trace, 0, length - 1, axis=elem_axis)], axis=elem_axis)
        high_outer = jnp.concatenate([lax.slice_in_dim(low_trace, 1, length, axis=elem_axis), jnp.expand_dims(upper_side, elem_axis)], axis=elem_axis)
        lifting = metric_grid[direction] * (0.5 / END_WEIGHT)
        wave_speed = abs(FLOW[direction]) + 1.0
        low_jump = low_outer - low_trace
        high_jump = high_outer - high_trace
        low_term = lifting * (flux_along(low_jump, direction) + wave_speed * low_jump)
        high_term = lifting * (wave_speed * high_jump - flux_along(high_jump, direction))
        picker = [slice(None)] * 7
        picker[node_axis] = 0
        tendency = tendency.at[tuple(picker)].add(low_term)
        picker[node_axis] = 5
        tendency = tendency.at[tuple(picker)].add(high_term)
    return tendency

def invert_order(placing):
    return jnp.zeros_like(placing).at[placing].set(jnp.arange(placing.shape[0], dtype=jnp.int32))

def to_global(values, width):
    shaped = values.reshape(2, SECTORS, BLOCKS, width, EL_C, EL_R, EL_A)
    shaped = jnp.transpose(shaped, (0, 3, 1, 4, 2, 5, 6))
    return shaped.reshape(2, width, SECTORS * EL_C, BLOCKS * EL_R, EL_A)

def from_global(values, width):
    shaped = values.reshape(2, width, SECTORS, EL_C, BLOCKS, EL_R, EL_A)
    shaped = jnp.transpose(shaped, (0, 2, 4, 1, 3, 5, 6))
    return shaped.reshape(2 * SECTORS * BLOCKS, width, ELEMS)

def reference(current, section_base, metric, slot_cell, rotation, mortar_index):
    blocks = 2 * SECTORS * BLOCKS
    columns = SECTORS * EL_C
    placing = slot_cell.reshape(blocks, ELEMS).astype(jnp.int32)
    inverse = jax.vmap(invert_order)(placing)
    values = jnp.take_along_axis(current.reshape(blocks, 5 * 216, ELEMS), inverse[:, None, :], axis=2)
    scales = jnp.take_along_axis(metric.reshape(blocks, 3, ELEMS), inverse[:, None, :], axis=2)
    global_grid = to_global(values, 5 * 216).reshape(2, 5, 6, 6, 6, columns, BLOCKS * EL_R, EL_A)
    global_metric = to_global(scales, 3)
    derivative = jnp.asarray(derivative_table(), dtype=jnp.float32)
    tables = jnp.asarray(mortar_tables(), dtype=jnp.float32)
    selected = tables[:, mortar_index]
    offset_value = rotation[0]
    rotor_face = global_grid[0][:, :, :, 5, :, :, -1]
    stator_face = global_grid[1][:, :, :, 0, :, :, 0]
    stator_outer = mix_columns(selected[1], jnp.roll(rotor_face, offset_value + 1, axis=3)) + mix_columns(selected[0], jnp.roll(rotor_face, offset_value, axis=3))
    rotor_outer = mix_columns(selected[2], jnp.roll(stator_face, -offset_value, axis=3)) + mix_columns(selected[3], jnp.roll(stator_face, -offset_value - 1, axis=3))
    radial_zero = jnp.zeros((5, 6, 6, columns, EL_A), dtype=jnp.float32)
    axial_zero = jnp.zeros((5, 6, 6, columns, BLOCKS * EL_R), dtype=jnp.float32)
    tendencies = []
    for side_number in range(2):
        field_grid = global_grid[side_number]
        circ_pair = (field_grid[:, 5, :, :, -1], field_grid[:, 0, :, :, 0])
        if side_number == 0:
            axial_pair = (axial_zero, rotor_outer)
        else:
            axial_pair = (stator_outer, axial_zero)
        tendencies.append(time_rate(field_grid, global_metric[side_number], derivative, [circ_pair, (radial_zero, radial_zero), axial_pair]))
    stacked = jnp.stack(tendencies).reshape(2, 5 * 216, columns, BLOCKS * EL_R, EL_A)
    slotted = jnp.take_along_axis(from_global(stacked, 5 * 216), placing[:, None, :], axis=2)
    slotted = slotted.reshape(current.shape)
    return 0.75 * section_base + 0.25 * (current + STEP * slotted)
```

```python
import functools
import math

import jax
import jax.numpy as jnp
import numpy as np
from jax import lax
from jax.experimental import pallas as pl
from jax.experimental.pallas import tpu as pltpu
from jax.sharding import PartitionSpec as P

EL_C = 8
EL_R = 4
EL_A = 8
FRACS = 8
ELEMS = 256
NODES = 216
FIELDS = 5
STRIP = EL_R * EL_A

FLOW = (0.3, -0.2, 0.25)
WAVE = tuple(abs(u) + 1.0 for u in FLOW)
LIFT = 7.5
STEP = 0.02
WEIGHT = 0.25 * STEP

FACE = 40
IFACE = 48
FACES = 4 * FACE + 2 * IFACE
CIRC_ROWS = 56
RADIAL_ROWS = 104
INTER_ROWS = 64


def node_table():
    inner_point = math.sqrt(1.0 / 3.0 - 2.0 * math.sqrt(7.0) / 21.0)
    outer_point = math.sqrt(1.0 / 3.0 + 2.0 * math.sqrt(7.0) / 21.0)
    return np.array([-1.0, -outer_point, -inner_point, inner_point, outer_point, 1.0])


def derivative_table():
    abscissa = node_table()
    weights_bary = np.array(
        [np.prod([abscissa[i] - abscissa[m] for m in range(6) if m != i]) for i in range(6)]
    )
    matrix = np.zeros((6, 6))
    for i in range(6):
        for j in range(6):
            if i != j:
                matrix[i, j] = weights_bary[i] / (weights_bary[j] * (abscissa[i] - abscissa[j]))
        matrix[i, i] = -np.sum(matrix[i])
    return matrix


def basis_values(points):
    nodes_unit = (node_table() + 1.0) / 2.0
    values = np.ones((points.shape[0], 6))
    for j in range(6):
        for m in range(6):
            if m != j:
                values[:, j] = (
                    values[:, j] * (points - nodes_unit[m]) / (nodes_unit[j] - nodes_unit[m])
                )
    return values


def mortar_tables():
    nodes_unit = (node_table() + 1.0) / 2.0
    tables = np.zeros((4, FRACS, 6, 6))
    for k in range(FRACS):
        fraction = k / FRACS
        beyond = nodes_unit >= fraction
        tables[0, k] = np.where(beyond[:, None], basis_values(nodes_unit - fraction), 0.0)
        tables[1, k] = np.where(beyond[:, None], 0.0, basis_values(nodes_unit - fraction + 1.0))
        crossing = nodes_unit + fraction >= 1.0
        tables[2, k] = np.where(crossing[:, None], 0.0, basis_values(nodes_unit + fraction))
        tables[3, k] = np.where(crossing[:, None], basis_values(nodes_unit + fraction - 1.0), 0.0)
    return tables


def split_np(values):
    high = values.astype(jnp.bfloat16)
    low = (values - high.astype(np.float64)).astype(jnp.bfloat16)
    return high, low


def operator_rows():
    one = -derivative_table()
    one[0, 0] -= LIFT
    one[5, 5] += LIFT
    rows = np.zeros((3, 2, 16, ELEMS))
    nodes = np.arange(NODES)
    for direction, stride in enumerate((36, 6, 1)):
        for part, values in enumerate(split_np(one)):
            rows[direction, part, :6, :NODES] = values.astype(np.float64)[:, nodes // stride % 6]
    return rows


def over(values, divisor):
    return jnp.right_shift(values * (-(-65536 // divisor)), 16)


def face_node(row):
    face = over(row, FACE)
    place = row - face * FACE
    major = over(place, 6)
    minor = place - 6 * major
    circ = jnp.where(face == 1, 180, 0) + place
    radial = jnp.where(face == 3, 30, 0) + 36 * major + minor
    node = jnp.where(face < 2, circ, radial)
    node = jnp.where(place < 36, node, -1)
    spot = row - 4 * FACE
    upper = spot >= IFACE
    spot = spot - jnp.where(upper, IFACE, 0)
    major = jnp.right_shift(spot, 3)
    minor = spot - 8 * major
    axial = 36 * major + 6 * minor + jnp.where(upper, 5, 0)
    axial = jnp.where(minor < 6, axial, -1)
    return jnp.where(row < 4 * FACE, node, axial)


def mortar_columns():
    tables = mortar_tables().reshape(4, FRACS, 36)
    table = np.zeros((80, 16))
    for k in range(FRACS):
        table[:36, k] = tables[2, k]
        table[40:76, k] = tables[3, k]
        table[:36, 8 + k] = tables[1, k]
        table[40:76, 8 + k] = tables[0, k]
    high = table.astype(jnp.bfloat16)
    rest = table - high.astype(np.float64)
    middle = rest.astype(jnp.bfloat16)
    low = (rest - middle.astype(np.float64)).astype(jnp.bfloat16)
    return np.concatenate([high, middle, low], axis=1)


def mm(a, b):
    return jnp.dot(a, b, preferred_element_type=jnp.float32)


def split(values):
    high = values.astype(jnp.bfloat16)
    low = (values - high.astype(jnp.float32)).astype(jnp.bfloat16)
    return high, low


def mm_split(values, table):
    high, low = split(values)
    return mm(high, table) + mm(low, table)


def hits(a, b):
    return (a == b).astype(jnp.float32).astype(jnp.bfloat16)


def cell_column(cell):
    rows = jnp.broadcast_to(cell.astype(jnp.float32), (8, ELEMS))
    return jnp.transpose(rows)[:, 0:1].astype(jnp.int32)


def border_cells(kind, index):
    if kind == "circ_low":
        return index
    if kind == "circ_high":
        return index + (EL_C - 1) * STRIP
    if kind == "radial_low":
        return (index // EL_A) * STRIP + index % EL_A
    if kind == "radial_high":
        return (index // EL_A) * STRIP + index % EL_A + (EL_R - 1) * EL_A
    return index * EL_A


def lanes_of(parts, width, rows):
    lane = lax.broadcasted_iota(jnp.int32, (rows, 128), 1) // width
    packed = parts[0:rows]
    for j in range(1, 128 // width):
        packed = jnp.where(lane == j, parts[j * rows : (j + 1) * rows], packed)
    return packed


def rows_of(packed, width, rows):
    lane = lax.broadcasted_iota(jnp.int32, (rows, 128), 1) // width
    return jnp.concatenate(
        [jnp.where(lane == j, packed, 0.0) for j in range(128 // width)], axis=0
    )


def start_all(pairs, sems):
    copies = [pltpu.make_async_copy(src, dst, sems.at[k]) for k, (src, dst) in enumerate(pairs)]
    for copy in copies:
        copy.start()
    return copies


def pack_kernel(
    current,
    cell_ref,
    inter,
    circ_low,
    circ_high,
    radial_low,
    radial_high,
    fields,
    traces,
    lifter,
    cells,
    sems,
):
    side = lax.axis_index("side")
    copies = start_all(
        [(cell_ref, cells)] + [(current.at[f], fields.at[f]) for f in range(FIELDS)], sems
    )
    iota = lax.broadcasted_iota
    node = face_node(iota(jnp.int32, (FACES, 1), 0))
    faces = hits(node, iota(jnp.int32, (FACES, NODES), 1))
    lifter[...] = hits(iota(jnp.int32, (NODES, FACES), 0), face_node(iota(jnp.int32, (1, FACES), 1)))
    lane = iota(jnp.int32, (ELEMS, 128), 1)
    jobs = (
        (circ_low, "circ_low", 0, FACE, 32, CIRC_ROWS),
        (circ_high, "circ_high", FACE, FACE, 32, CIRC_ROWS),
        (radial_low, "radial_low", 2 * FACE, FACE, 64, RADIAL_ROWS),
        (radial_high, "radial_high", 3 * FACE, FACE, 64, RADIAL_ROWS),
        (inter, "inter", 4 * FACE, IFACE, 32, INTER_ROWS),
    )
    copies[0].wait()
    column = cell_column(cells[...])
    tables = []
    for out, kind, start, count, width, block in jobs:
        wanted = border_cells(kind, lane % width)
        if kind == "inter":
            wanted = wanted + (EL_A - 1) * (1 - side)
        tables.append(hits(column, wanted))
    for f in range(FIELDS):
        copies[1 + f].wait()
        high, low = split(fields[f])
        traces[f] = mm(faces, high) + mm(faces, low)

    def rows(start, count, total):
        if start == 4 * FACE:
            parts = [
                jnp.where(side == 0, traces[f, start + count :], traces[f, start : start + count])
                for f in range(FIELDS)
            ]
        else:
            parts = [traces[f, start : start + count] for f in range(FIELDS)]
        extra = total - FIELDS * count
        if extra:
            parts.append(jnp.zeros((extra, ELEMS), jnp.float32))
        return jnp.concatenate(parts, axis=0)

    for table, (out, kind, start, count, width, block) in zip(tables, jobs):
        values = mm_split(rows(start, count, block * (128 // width)), table)
        out[...] = lanes_of(values, width, block)


def jump_terms(exterior, direction, sign, scale):
    first = (WAVE[direction] - sign * FLOW[direction]) * scale
    second = sign * scale
    terms = [first * e for e in exterior]
    terms[0] = terms[0] - second * exterior[1 + direction]
    terms[1 + direction] = terms[1 + direction] - second * exterior[0]
    return terms


def volume_kernel(
    fields,
    traces,
    lifter,
    base,
    metric,
    cell_ref,
    rows_hbm,
    result,
    bases,
    metrics,
    cells,
    rows,
    sems,
):
    copies = start_all(
        [(rows_hbm, rows), (metric, metrics), (cell_ref, cells)]
        + [(base.at[f], bases.at[f]) for f in range(FIELDS)],
        sems,
    )
    iota = lax.broadcasted_iota
    column = iota(jnp.int32, (NODES, 1), 0)
    line = iota(jnp.int32, (1, ELEMS), 1)
    lane = iota(jnp.int32, (NODES, 16), 1)

    def indices(node):
        circ = over(node, 36)
        major = over(node, 6)
        return circ, major - 6 * circ, node - 6 * major

    own_index = indices(column)
    line_index = indices(line)
    waves = jnp.zeros((NODES, 16), jnp.float32)
    chosen = []
    alike = []
    for d, stride in enumerate((36, 6, 1)):
        end = (own_index[d] == 0) | (own_index[d] == 5)
        strength = jnp.where(end, -LIFT * WAVE[d], 0.0)
        waves = waves + jnp.where(lane % 8 == d, strength, 0.0)
        chosen.append(hits(lane, own_index[d]))
        alike.append(column - stride * own_index[d] == line - stride * line_index[d])
    copies[0].wait()
    op_high = []
    op_low = []
    for d in range(3):
        for part, out in ((0, op_high), (1, op_low)):
            spread = jnp.where(alike[d], mm(chosen[d], rows[d, part]), 0.0)
            out.append(spread[:, :NODES].astype(jnp.bfloat16))
    copies[1].wait()
    copies[2].wait()
    scale = [metrics[d] * WEIGHT for d in range(3)]
    scaled = jnp.concatenate(scale, axis=0)
    cell = cells[...]
    cell_rows = cell_column(cell)
    filler = jnp.zeros((5, ELEMS), jnp.float32)
    scale_high = scaled.astype(jnp.bfloat16).astype(jnp.float32)
    scale_rows = jnp.concatenate([scaled, filler, scaled - scale_high, filler], axis=0)
    diagonal = 0.25 + mm(waves.astype(jnp.bfloat16), scale_rows.astype(jnp.bfloat16))
    own = []
    for f in range(FIELDS):
        u = fields[f]
        high, low = split(u)
        rates = [
            mm(op_high[d], high) + mm(op_high[d], low) + mm(op_low[d], high) for d in range(3)
        ]
        copies[3 + f].wait()
        total = 0.75 * bases[f] + diagonal * u
        for d in range(3):
            total = total + (FLOW[d] * scale[d]) * rates[d]
        if f == 0:
            pressure = rates
        elif f < 4:
            total = total + scale[f - 1] * pressure[f - 1]
            own[0] = own[0] + scale[f - 1] * rates[f - 1]
        own.append(total)
    place = (cell // STRIP, cell // EL_A % EL_R, cell % EL_A)
    length = (EL_C, EL_R, EL_A)
    stride = (STRIP, EL_A, 1)
    terms = [[] for _ in range(FIELDS)]
    for d in range(3):
        for end in range(2):
            if end == 0:
                wanted = jnp.where(place[d] == 0, -1, cell - stride[d])
            else:
                wanted = jnp.where(place[d] == length[d] - 1, -1, cell + stride[d])
            table = hits(cell_rows, wanted)
            count = IFACE if d == 2 else FACE
            start = 2 * d * FACE + (1 - end) * count
            trace = [traces[f, start : start + count] for f in range(FIELDS)]
            outer = mm_split(jnp.concatenate(trace, axis=0), table)
            outer = [outer[f * count : (f + 1) * count] for f in range(FIELDS)]
            found = jump_terms(outer, d, 2.0 * end - 1.0, LIFT * scale[d])
            for f in range(FIELDS):
                terms[f].append(found[f])
    for f in range(FIELDS):
        high, low = split(jnp.concatenate(terms[f], axis=0))
        result[f] = own[f] + mm(lifter[...], high) + mm(lifter[...], low)


def border_kernel(
    rotation,
    mortar,
    partial,
    lifter,
    near,
    far,
    from_low,
    from_high,
    from_below,
    from_above,
    metric_hbm,
    cell_hbm,
    coefficients_hbm,
    out,
    metrics,
    cells,
    coefficients,
    result,
    sems,
    out_sems,
):
    side = lax.axis_index("side")
    radial = lax.axis_index("radial")
    copies = start_all(
        [(cell_hbm, cells), (metric_hbm, metrics), (coefficients_hbm, coefficients)], sems
    )
    for copy in copies:
        copy.wait()
    cell = cells[...]
    scale = [metrics[d] * (WEIGHT * LIFT) for d in range(3)]
    row = lax.broadcasted_iota(jnp.int32, (ELEMS, ELEMS), 0) % 128
    jobs = (
        (from_low, "circ_low", 0, 0, 32, CIRC_ROWS),
        (from_high, "circ_high", 0, 1, 32, CIRC_ROWS),
        (from_below, "radial_low", 1, 0, 64, RADIAL_ROWS),
        (from_above, "radial_high", 1, 1, 64, RADIAL_ROWS),
    )
    tables = [hits(border_cells(kind, row % width), cell) for _, kind, _, _, width, _ in jobs]
    remainder = rotation[0] % EL_C
    first = jnp.where(side == 0, remainder, EL_C - 1 - remainder)
    radial_place = cell // EL_A % EL_R
    facing = cell % EL_A == (EL_A - 1) * (1 - side)
    pickers = []
    for later in range(2):
        at = cell // STRIP + first + later
        index = at * EL_R + radial_place
        early_index = jnp.where(facing & (at < EL_C), index, -1)
        late_index = jnp.where(facing & (at >= EL_C), index - EL_C * EL_R, -1)
        pickers.append((hits(row % 32, early_index), hits(row % 32, late_index)))
    fraction = jnp.zeros_like(cell)
    for r in range(EL_R):
        fraction = jnp.where(radial_place == r, mortar[r], fraction)
    chosen = lax.broadcasted_iota(jnp.int32, (48, ELEMS), 0) % 16 == fraction + 8 * side
    weights = mm(coefficients[...], chosen.astype(jnp.float32).astype(jnp.bfloat16))

    def both(values):
        high = values.astype(jnp.bfloat16).astype(jnp.float32)
        return jnp.concatenate([high, values - high], axis=1).astype(jnp.bfloat16)

    terms = [[] for _ in range(FIELDS)]
    for table, (source, kind, d, end, width, block) in zip(tables, jobs):
        outer = mm(both(rows_of(source[...], width, block)), table)
        outer = [outer[f * FACE : (f + 1) * FACE] for f in range(FIELDS)]
        factor = scale[d]
        if d == 1:
            wall = 0 if end == 0 else 3
            factor = factor * jnp.where(radial == wall, 0.0, 1.0)
        found = jump_terms(outer, d, 2.0 * end - 1.0, factor)
        for f in range(FIELDS):
            terms[f].append(found[f])
    earlier = jnp.where(side == 0, near[...], far[...])
    later = jnp.where(side == 0, far[...], near[...])
    earlier_parts = both(rows_of(earlier, 32, INTER_ROWS))
    later_parts = both(rows_of(later, 32, INTER_ROWS))
    windows = [mm(earlier_parts, a) + mm(later_parts, b) for a, b in pickers]
    outer = []
    for f in range(FIELDS):
        blocks = []
        for i in range(6):
            total = None
            for later in range(2):
                for j in range(6):
                    at = 40 * later + 6 * i + j
                    start = f * IFACE + 8 * j
                    part = weights[at : at + 1] * windows[later][start : start + 8]
                    total = part if total is None else total + part
            blocks.append(total)
        outer.append(jnp.concatenate(blocks, axis=0))
    sign = jnp.where(side == 0, 1.0, -1.0)
    found = jump_terms(outer, 2, sign, scale[2])
    stores = []
    for f in range(FIELDS):
        terms[f].append(jnp.where(side == 1, found[f], 0.0))
        terms[f].append(jnp.where(side == 0, found[f], 0.0))
        high, low = split(jnp.concatenate(terms[f], axis=0))
        table = lifter[...]
        result[f] = partial[f] + mm(table, high) + mm(table, low)
        stores.append(pltpu.make_async_copy(result.at[f], out.at[f], out_sems.at[f]))
        stores[f].start()
    for store in stores:
        store.wait()


def to_partner(shift):
    def send(block):
        pairs = []
        for k in range(32):
            other = (k + shift) % 32
            pairs += [(2 * k, 2 * other + 1), (2 * other + 1, 2 * k)]
        return lax.ppermute(block, ("circ", "side"), pairs)

    return send


def to_beside(block):
    pairs = []
    for k in range(32):
        pairs += [(2 * k, 2 * ((k - 1) % 32)), (2 * k + 1, 2 * ((k + 1) % 32) + 1)]
    return lax.ppermute(block, ("circ", "side"), pairs)


def ring(block, axis, step):
    count = lax.axis_size(axis)
    return lax.ppermute(block, axis, [(i, (i + step) % count) for i in range(count)])


def constant(values):
    return jnp.asarray(np.asarray(values), dtype=jnp.bfloat16)


def local(current, section_base, metric, slot_cell, rotation, mortar_index):
    current = current.reshape(FIELDS, NODES, ELEMS)
    section_base = section_base.reshape(FIELDS, NODES, ELEMS)
    metric = metric.reshape(3, 1, ELEMS)
    cell = slot_cell.reshape(1, ELEMS)
    params = pltpu.CompilerParams(vmem_limit_bytes=24 * 1024 * 1024)
    smem = pl.BlockSpec(memory_space=pltpu.SMEM)
    vmem = pl.BlockSpec(memory_space=pltpu.VMEM)
    anywhere = pl.BlockSpec(memory_space=pl.ANY)
    whole = (FIELDS, NODES, ELEMS)

    def buffer(*dims, kind=jnp.float32):
        return pltpu.VMEM(dims, kind)

    current, section_base, metric, cell = (
        pltpu.with_memory_space_constraint(x, pltpu.HBM)
        for x in (current, section_base, metric, cell)
    )
    inter, circ_low, circ_high, radial_low, radial_high, fields, traces, lifter = pl.pallas_call(
        pack_kernel,
        in_specs=[anywhere] * 2,
        out_specs=[vmem] * 8,
        out_shape=[
            buffer(INTER_ROWS, 128),
            buffer(CIRC_ROWS, 128),
            buffer(CIRC_ROWS, 128),
            buffer(RADIAL_ROWS, 128),
            buffer(RADIAL_ROWS, 128),
            buffer(*whole),
            buffer(FIELDS, FACES, ELEMS),
            buffer(NODES, FACES, kind=jnp.bfloat16),
        ],
        scratch_shapes=[
            buffer(1, ELEMS, kind=jnp.int32),
            pltpu.SemaphoreType.DMA((1 + FIELDS,)),
        ],
        compiler_params=params,
        name="pack",
    )(current, cell)
    near = lax.switch(
        jnp.right_shift(rotation[0], 3), [to_partner(k) for k in range(32)], inter
    )
    far = to_beside(near)
    from_low = ring(circ_high, "circ", 1)
    from_high = ring(circ_low, "circ", -1)
    from_below = ring(radial_high, "radial", 1)
    from_above = ring(radial_low, "radial", -1)
    partial = pl.pallas_call(
        volume_kernel,
        in_specs=[vmem] * 3 + [anywhere] * 4,
        out_specs=vmem,
        out_shape=buffer(*whole),
        scratch_shapes=[
            buffer(*whole),
            buffer(3, 1, ELEMS),
            buffer(1, ELEMS, kind=jnp.int32),
            buffer(3, 2, 16, ELEMS, kind=jnp.bfloat16),
            pltpu.SemaphoreType.DMA((3 + FIELDS,)),
        ],
        compiler_params=params,
        cost_estimate=pl.CostEstimate(
            flops=4 * 10**9, bytes_accessed=4 * 10**6, transcendentals=0
        ),
        name="volume",
    )(fields, traces, lifter, section_base, metric, cell, constant(operator_rows()))
    out = pl.pallas_call(
        border_kernel,
        in_specs=[smem, smem] + [vmem] * 8 + [anywhere] * 3,
        out_specs=anywhere,
        out_shape=jax.ShapeDtypeStruct(whole, jnp.float32),
        scratch_shapes=[
            buffer(3, 1, ELEMS),
            buffer(1, ELEMS, kind=jnp.int32),
            buffer(80, 48, kind=jnp.bfloat16),
            buffer(*whole),
            pltpu.SemaphoreType.DMA((3,)),
            pltpu.SemaphoreType.DMA((FIELDS,)),
        ],
        compiler_params=params,
        name="border",
    )(
        rotation,
        mortar_index,
        partial,
        lifter,
        near,
        far,
        from_low,
        from_high,
        from_below,
        from_above,
        metric,
        cell,
        constant(mortar_columns()),
    )
    return out.reshape(1, 1, 1, FIELDS, NODES, ELEMS)


def solution(mesh):
    return jax.shard_map(
        local,
        mesh=mesh,
        in_specs=(
            P("side", "circ", "radial", None, None, None),
            P("side", "circ", "radial", None, None, None),
            P("side", "circ", "radial", None, None),
            P("side", "circ", "radial", None),
            P(),
            P("radial"),
        ),
        out_specs=P("side", "circ", "radial", None, None, None),
        check_vma=False,
    )
```

```python
import functools
import math

import jax
import jax.numpy as jnp
import numpy as np
from jax import lax
from jax.experimental import pallas as pl
from jax.experimental.pallas import tpu as pltpu
from jax.sharding import PartitionSpec as P

EL_C = 8
EL_R = 4
EL_A = 8
FRACS = 8
ELEMS = 256
NODES = 216
FIELDS = 5
STRIP = EL_R * EL_A

FLOW = (0.3, -0.2, 0.25)
WAVE = tuple(abs(u) + 1.0 for u in FLOW)
LIFT = 7.5
STEP = 0.02
WEIGHT = 0.25 * STEP

FACE = 40
IFACE = 48
FACES = 4 * FACE + 2 * IFACE
CIRC_ROWS = 56
RADIAL_ROWS = 104
INTER_ROWS = 64
PIECE = 224


def node_table():
    inner_point = math.sqrt(1.0 / 3.0 - 2.0 * math.sqrt(7.0) / 21.0)
    outer_point = math.sqrt(1.0 / 3.0 + 2.0 * math.sqrt(7.0) / 21.0)
    return np.array([-1.0, -outer_point, -inner_point, inner_point, outer_point, 1.0])


def derivative_table():
    abscissa = node_table()
    weights_bary = np.array(
        [np.prod([abscissa[i] - abscissa[m] for m in range(6) if m != i]) for i in range(6)]
    )
    matrix = np.zeros((6, 6))
    for i in range(6):
        for j in range(6):
            if i != j:
                matrix[i, j] = weights_bary[i] / (weights_bary[j] * (abscissa[i] - abscissa[j]))
        matrix[i, i] = -np.sum(matrix[i])
    return matrix


def basis_values(points):
    nodes_unit = (node_table() + 1.0) / 2.0
    values = np.ones((points.shape[0], 6))
    for j in range(6):
        for m in range(6):
            if m != j:
                values[:, j] = (
                    values[:, j] * (points - nodes_unit[m]) / (nodes_unit[j] - nodes_unit[m])
                )
    return values


def mortar_tables():
    nodes_unit = (node_table() + 1.0) / 2.0
    tables = np.zeros((4, FRACS, 6, 6))
    for k in range(FRACS):
        fraction = k / FRACS
        beyond = nodes_unit >= fraction
        tables[0, k] = np.where(beyond[:, None], basis_values(nodes_unit - fraction), 0.0)
        tables[1, k] = np.where(beyond[:, None], 0.0, basis_values(nodes_unit - fraction + 1.0))
        crossing = nodes_unit + fraction >= 1.0
        tables[2, k] = np.where(crossing[:, None], 0.0, basis_values(nodes_unit + fraction))
        tables[3, k] = np.where(crossing[:, None], basis_values(nodes_unit + fraction - 1.0), 0.0)
    return tables


def split_np(values):
    high = values.astype(jnp.bfloat16)
    low = (values - high.astype(np.float64)).astype(jnp.bfloat16)
    return high, low


def node_operators():
    one = -derivative_table()
    one[0, 0] -= LIFT
    one[5, 5] += LIFT
    eye = np.eye(6)
    table = np.zeros((6 * NODES, PIECE))
    for direction in range(3):
        parts = [eye, eye, eye]
        parts[direction] = one
        for half, values in enumerate(split_np(np.kron(np.kron(parts[0], parts[1]), parts[2]))):
            start = (3 * half + direction) * NODES
            table[start : start + NODES, :NODES] = values
    return table


def wave_columns():
    columns = np.zeros((NODES, 16))
    nodes = np.arange(NODES)
    for direction, stride in enumerate((36, 6, 1)):
        ends = nodes // stride % 6 % 5 == 0
        columns[:, direction] = -LIFT * WAVE[direction] * ends
        columns[:, 8 + direction] = columns[:, direction]
    return columns


def over(values, divisor):
    return jnp.right_shift(values * (-(-65536 // divisor)), 16)


def face_node(row):
    face = over(row, FACE)
    place = row - face * FACE
    major = over(place, 6)
    minor = place - 6 * major
    circ = jnp.where(face == 1, 180, 0) + place
    radial = jnp.where(face == 3, 30, 0) + 36 * major + minor
    node = jnp.where(face < 2, circ, radial)
    node = jnp.where(place < 36, node, -1)
    spot = row - 4 * FACE
    upper = spot >= IFACE
    spot = spot - jnp.where(upper, IFACE, 0)
    major = jnp.right_shift(spot, 3)
    minor = spot - 8 * major
    axial = 36 * major + 6 * minor + jnp.where(upper, 5, 0)
    axial = jnp.where(minor < 6, axial, -1)
    return jnp.where(row < 4 * FACE, node, axial)


def mortar_columns():
    tables = mortar_tables().reshape(4, FRACS, 36)
    table = np.zeros((80, 16))
    for k in range(FRACS):
        table[:36, k] = tables[2, k]
        table[40:76, k] = tables[3, k]
        table[:36, 8 + k] = tables[1, k]
        table[40:76, 8 + k] = tables[0, k]
    high = table.astype(jnp.bfloat16)
    rest = table - high.astype(np.float64)
    middle = rest.astype(jnp.bfloat16)
    low = (rest - middle.astype(np.float64)).astype(jnp.bfloat16)
    return np.concatenate([high, middle, low], axis=1)


def mm(a, b):
    return jnp.dot(a, b, preferred_element_type=jnp.float32)


def split(values):
    high = values.astype(jnp.bfloat16)
    low = (values - high.astype(jnp.float32)).astype(jnp.bfloat16)
    return high, low


def mm_split(values, table):
    rows = values.shape[0]
    high = values.astype(jnp.bfloat16).astype(jnp.float32)
    both = jnp.concatenate([high, values - high], axis=0).astype(jnp.bfloat16)
    product = mm(both, table)
    return product[:rows] + product[rows:]


def lift(lifter, terms):
    high, low = split(jnp.concatenate(terms, axis=0))
    return mm(jnp.concatenate([lifter, lifter], axis=1), jnp.concatenate([high, low], axis=0))


def hits(a, b):
    return (a == b).astype(jnp.float32).astype(jnp.bfloat16)


def cell_column(cell):
    rows = jnp.broadcast_to(cell.astype(jnp.float32), (8, ELEMS))
    return jnp.transpose(rows)[:, 0:1].astype(jnp.int32)


def border_cells(kind, index):
    if kind == "circ_low":
        return index
    if kind == "circ_high":
        return index + (EL_C - 1) * STRIP
    if kind == "radial_low":
        return (index // EL_A) * STRIP + index % EL_A
    if kind == "radial_high":
        return (index // EL_A) * STRIP + index % EL_A + (EL_R - 1) * EL_A
    return index * EL_A


def lanes_of(parts, width, rows):
    lane = lax.broadcasted_iota(jnp.int32, (rows, 128), 1) // width
    packed = parts[0:rows]
    for j in range(1, 128 // width):
        packed = jnp.where(lane == j, parts[j * rows : (j + 1) * rows], packed)
    return packed


def rows_of(packed, width, rows):
    lane = lax.broadcasted_iota(jnp.int32, (rows, 128), 1) // width
    return jnp.concatenate(
        [jnp.where(lane == j, packed, 0.0) for j in range(128 // width)], axis=0
    )


def start_all(pairs, sems):
    copies = [pltpu.make_async_copy(src, dst, sems.at[k]) for k, (src, dst) in enumerate(pairs)]
    for copy in copies:
        copy.start()
    return copies


def pack_kernel(
    current,
    cell_ref,
    metric,
    operators_hbm,
    inter,
    circ_low,
    circ_high,
    radial_low,
    radial_high,
    pieces,
    traces,
    operators,
    cells,
    metrics,
    fields,
    sems,
):
    side = lax.axis_index("side")
    copies = start_all(
        [(cell_ref, cells), (metric, metrics)]
        + [(current.at[f], fields.at[f]) for f in range(FIELDS)]
        + [(operators_hbm, operators)],
        sems,
    )
    iota = lax.broadcasted_iota
    spot = iota(jnp.int32, (1, 2 * PIECE), 1)
    spot = jnp.where(spot >= PIECE, spot - PIECE, spot)
    faces = hits(face_node(iota(jnp.int32, (FACES, 1), 0)), spot)
    copies[0].wait()
    column = jnp.broadcast_to(cell_column(cells[...]), (ELEMS, 128))
    line = iota(jnp.int32, (1, 128), 1)
    jobs = (
        (circ_low, "circ_low", 0, FACE, 32, CIRC_ROWS),
        (circ_high, "circ_high", FACE, FACE, 32, CIRC_ROWS),
        (radial_low, "radial_low", 2 * FACE, FACE, 64, RADIAL_ROWS),
        (radial_high, "radial_high", 3 * FACE, FACE, 64, RADIAL_ROWS),
        (inter, "inter", 4 * FACE, IFACE, 32, INTER_ROWS),
    )
    tables = []
    for out, kind, start, count, width, block in jobs:
        wanted = border_cells(kind, line % width)
        if kind == "inter":
            wanted = wanted + (EL_A - 1) * (1 - side)
        tables.append(hits(column, wanted))
    copies[1].wait()
    filler = jnp.zeros((PIECE - NODES, ELEMS), jnp.float32)
    for f in range(FIELDS):
        copies[2 + f].wait()
        high, low = split(jnp.concatenate([fields[f], filler], axis=0))
        both = jnp.concatenate([high, low], axis=0)
        pieces[f] = both
        traces[f] = mm(faces, both)

    def rows(start, count, total):
        if start == 4 * FACE:
            parts = [
                jnp.where(side == 0, traces[f, start + count :], traces[f, start : start + count])
                for f in range(FIELDS)
            ]
        else:
            parts = [traces[f, start : start + count] for f in range(FIELDS)]
        extra = total - FIELDS * count
        if extra:
            parts.append(jnp.zeros((extra, ELEMS), jnp.float32))
        return jnp.concatenate(parts, axis=0)

    for table, (out, kind, start, count, width, block) in zip(tables, jobs):
        values = mm_split(rows(start, count, block * (128 // width)), table)
        out[...] = lanes_of(values, width, block)
    copies[-1].wait()


def jump_terms(exterior, direction, sign, scale):
    first = (WAVE[direction] - sign * FLOW[direction]) * scale
    second = sign * scale
    terms = [first * e for e in exterior]
    terms[0] = terms[0] - second * exterior[1 + direction]
    terms[1 + direction] = terms[1 + direction] - second * exterior[0]
    return terms


def volume_kernel(
    pieces,
    traces,
    operators,
    cells,
    metrics,
    waves_hbm,
    base,
    result,
    lifter,
    waves,
    bases,
    sems,
):
    copies = start_all(
        [(waves_hbm, waves)] + [(base.at[f], bases.at[f]) for f in range(FIELDS)], sems
    )
    iota = lax.broadcasted_iota
    lifter[...] = hits(iota(jnp.int32, (NODES, FACES), 0), face_node(iota(jnp.int32, (1, FACES), 1)))
    scale = [metrics[d] * WEIGHT for d in range(3)]
    cell = cells[...]
    cell_rows = jnp.broadcast_to(cell_column(cell), (ELEMS, ELEMS))
    place = (cell // STRIP, cell // EL_A % EL_R, cell % EL_A)
    length = (EL_C, EL_R, EL_A)
    stride = (STRIP, EL_A, 1)
    terms = [[] for _ in range(FIELDS)]
    for d in range(3):
        for end in range(2):
            if end == 0:
                wanted = jnp.where(place[d] == 0, -1, cell - stride[d])
            else:
                wanted = jnp.where(place[d] == length[d] - 1, -1, cell + stride[d])
            table = hits(cell_rows, wanted)
            count = IFACE if d == 2 else FACE
            start = 2 * d * FACE + (1 - end) * count
            trace = [traces[f, start : start + count] for f in range(FIELDS)]
            outer = mm_split(jnp.concatenate(trace, axis=0), table)
            outer = [outer[f * count : (f + 1) * count] for f in range(FIELDS)]
            found = jump_terms(outer, d, 2.0 * end - 1.0, LIFT * scale[d])
            for f in range(FIELDS):
                terms[f].append(found[f])
    copies[0].wait()
    scaled = jnp.concatenate(scale, axis=0)
    filler = jnp.zeros((5, ELEMS), jnp.float32)
    scale_high = scaled.astype(jnp.bfloat16).astype(jnp.float32)
    scale_rows = jnp.concatenate([scaled, filler, scaled - scale_high, filler], axis=0)
    diagonal = 0.25 + mm(waves[...], scale_rows.astype(jnp.bfloat16))
    own = []
    for f in range(FIELDS):
        high = pieces[f, :PIECE]
        low = pieces[f, PIECE:]
        full = mm(operators[...], high)
        full = full[: 3 * NODES] + full[3 * NODES :] + mm(operators[: 3 * NODES], low)
        rates = [full[d * NODES : (d + 1) * NODES] for d in range(3)]
        field = high.astype(jnp.float32) + low.astype(jnp.float32)
        total = diagonal * field[:NODES] + lift(lifter[...], terms[f])
        for d in range(3):
            total = total + (FLOW[d] * scale[d]) * rates[d]
        if f == 0:
            pressure = rates
        elif f < 4:
            total = total + scale[f - 1] * pressure[f - 1]
            own[0] = own[0] + scale[f - 1] * rates[f - 1]
        own.append(total)
    for f in range(FIELDS):
        copies[1 + f].wait()
        result[f] = own[f] + 0.75 * bases[f]


def border_kernel(
    rotation,
    mortar,
    partial,
    lifter,
    near,
    far,
    from_low,
    from_high,
    from_below,
    from_above,
    metrics,
    cells,
    coefficients,
    out,
    result,
    out_sems,
):
    side = lax.axis_index("side")
    radial = lax.axis_index("radial")
    cell = cells[...]
    scale = [metrics[d] * (WEIGHT * LIFT) for d in range(3)]
    row = lax.broadcasted_iota(jnp.int32, (ELEMS, ELEMS), 0)
    row_of = {32: row % 32, 64: row % 64}
    circ_place = cell // STRIP
    radial_place = cell // EL_A % EL_R
    circ_index = cell % STRIP
    radial_index = circ_place * EL_A + cell % EL_A
    jobs = (
        (from_low, jnp.where(circ_place == 0, circ_index, -1), 0, 0, 32, CIRC_ROWS),
        (from_high, jnp.where(circ_place == EL_C - 1, circ_index, -1), 0, 1, 32, CIRC_ROWS),
        (from_below, jnp.where(radial_place == 0, radial_index, -1), 1, 0, 64, RADIAL_ROWS),
        (from_above, jnp.where(radial_place == EL_R - 1, radial_index, -1), 1, 1, 64, RADIAL_ROWS),
    )
    tables = [hits(row_of[width], index) for _, index, _, _, width, _ in jobs]
    remainder = rotation[0] % EL_C
    first = jnp.where(side == 0, remainder, EL_C - 1 - remainder)
    facing = cell % EL_A == (EL_A - 1) * (1 - side)
    pickers = []
    for later in range(2):
        at = circ_place + first + later
        index = at * EL_R + radial_place
        early_index = jnp.where(facing & (at < EL_C), index, -1)
        late_index = jnp.where(facing & (at >= EL_C), index - EL_C * EL_R, -1)
        pickers.append((hits(row_of[32], early_index), hits(row_of[32], late_index)))
    fraction = jnp.zeros_like(cell)
    for r in range(EL_R):
        fraction = jnp.where(radial_place == r, mortar[r], fraction)
    chosen = lax.broadcasted_iota(jnp.int32, (48, ELEMS), 0) % 16 == fraction + 8 * side
    weights = mm(coefficients[...], chosen.astype(jnp.float32).astype(jnp.bfloat16))

    def both(values):
        high = values.astype(jnp.bfloat16).astype(jnp.float32)
        return jnp.concatenate([high, values - high], axis=1).astype(jnp.bfloat16)

    terms = [[] for _ in range(FIELDS)]
    for table, (source, _, d, end, width, block) in zip(tables, jobs):
        outer = mm(both(rows_of(source[...], width, block)), table)
        outer = [outer[f * FACE : (f + 1) * FACE] for f in range(FIELDS)]
        factor = scale[d]
        if d == 1:
            wall = 0 if end == 0 else 3
            factor = factor * jnp.where(radial == wall, 0.0, 1.0)
        found = jump_terms(outer, d, 2.0 * end - 1.0, factor)
        for f in range(FIELDS):
            terms[f].append(found[f])
    earlier = jnp.where(side == 0, near[...], far[...])
    later = jnp.where(side == 0, far[...], near[...])
    earlier_parts = both(rows_of(earlier, 32, INTER_ROWS))
    later_parts = both(rows_of(later, 32, INTER_ROWS))
    windows = [mm(earlier_parts, a) + mm(later_parts, b) for a, b in pickers]
    outer = []
    for f in range(FIELDS):
        blocks = []
        for i in range(6):
            total = None
            for later in range(2):
                for j in range(6):
                    at = 40 * later + 6 * i + j
                    start = f * IFACE + 8 * j
                    part = weights[at : at + 1] * windows[later][start : start + 8]
                    total = part if total is None else total + part
            blocks.append(total)
        outer.append(jnp.concatenate(blocks, axis=0))
    sign = jnp.where(side == 0, 1.0, -1.0)
    found = jump_terms(outer, 2, sign, scale[2])
    stores = []
    for f in range(FIELDS):
        terms[f].append(jnp.where(side == 1, found[f], 0.0))
        terms[f].append(jnp.where(side == 0, found[f], 0.0))
        result[f] = partial[f] + lift(lifter[...], terms[f])
        stores.append(pltpu.make_async_copy(result.at[f], out.at[f], out_sems.at[f]))
        stores[f].start()
    for store in stores:
        store.wait()


def to_partner(shift):
    def send(block):
        pairs = []
        for k in range(32):
            other = (k + shift) % 32
            pairs += [(2 * k, 2 * other + 1), (2 * other + 1, 2 * k)]
        return lax.ppermute(block, ("circ", "side"), pairs)

    return send


def to_beside(block):
    pairs = []
    for k in range(32):
        pairs += [(2 * k, 2 * ((k - 1) % 32)), (2 * k + 1, 2 * ((k + 1) % 32) + 1)]
    return lax.ppermute(block, ("circ", "side"), pairs)


def ring(block, axis, step):
    count = lax.axis_size(axis)
    return lax.ppermute(block, axis, [(i, (i + step) % count) for i in range(count)])


def constant(values):
    return jnp.asarray(np.asarray(values), dtype=jnp.bfloat16)


def local(current, section_base, metric, slot_cell, rotation, mortar_index):
    current = current.reshape(FIELDS, NODES, ELEMS)
    section_base = section_base.reshape(FIELDS, NODES, ELEMS)
    metric = metric.reshape(3, 1, ELEMS)
    cell = slot_cell.reshape(1, ELEMS)
    params = pltpu.CompilerParams(vmem_limit_bytes=24 * 1024 * 1024)
    smem = pl.BlockSpec(memory_space=pltpu.SMEM)
    vmem = pl.BlockSpec(memory_space=pltpu.VMEM)
    anywhere = pl.BlockSpec(memory_space=pl.ANY)
    whole = (FIELDS, NODES, ELEMS)

    def buffer(*dims, kind=jnp.float32):
        return pltpu.VMEM(dims, kind)

    current, section_base, metric, cell = (
        pltpu.with_memory_space_constraint(x, pltpu.HBM)
        for x in (current, section_base, metric, cell)
    )
    operators = node_operators()
    packed = pl.pallas_call(
        pack_kernel,
        in_specs=[anywhere] * 4,
        out_specs=[vmem] * 10,
        out_shape=[
            buffer(INTER_ROWS, 128),
            buffer(CIRC_ROWS, 128),
            buffer(CIRC_ROWS, 128),
            buffer(RADIAL_ROWS, 128),
            buffer(RADIAL_ROWS, 128),
            buffer(FIELDS, 2 * PIECE, ELEMS, kind=jnp.bfloat16),
            buffer(FIELDS, FACES, ELEMS),
            buffer(*operators.shape, kind=jnp.bfloat16),
            buffer(1, ELEMS, kind=jnp.int32),
            buffer(3, 1, ELEMS),
        ],
        scratch_shapes=[
            buffer(*whole),
            pltpu.SemaphoreType.DMA((3 + FIELDS,)),
        ],
        compiler_params=params,
        name="pack",
    )(current, cell, metric, pltpu.with_memory_space_constraint(constant(operators), pltpu.HBM))
    inter, circ_low, circ_high, radial_low, radial_high = packed[:5]
    pieces, traces, operators, cells, metrics = packed[5:]
    from_low = ring(circ_high, "circ", 1)
    from_high = ring(circ_low, "circ", -1)
    from_below = ring(radial_high, "radial", 1)
    from_above = ring(radial_low, "radial", -1)
    near = lax.switch(
        jnp.right_shift(rotation[0], 3), [to_partner(k) for k in range(32)], inter
    )
    far = to_beside(near)
    metrics, near = lax.optimization_barrier((metrics, near))
    partial, lifter = pl.pallas_call(
        volume_kernel,
        in_specs=[vmem] * 5 + [anywhere] * 2,
        out_specs=[vmem] * 2,
        out_shape=[buffer(*whole), buffer(NODES, FACES, kind=jnp.bfloat16)],
        scratch_shapes=[
            buffer(NODES, 16, kind=jnp.bfloat16),
            buffer(*whole),
            pltpu.SemaphoreType.DMA((1 + FIELDS,)),
        ],
        compiler_params=params,
        cost_estimate=pl.CostEstimate(
            flops=4 * 10**9, bytes_accessed=4 * 10**6, transcendentals=0
        ),
        name="volume",
    )(
        pieces,
        traces,
        operators,
        cells,
        metrics,
        pltpu.with_memory_space_constraint(constant(wave_columns()), pltpu.HBM),
        section_base,
    )
    out = pl.pallas_call(
        border_kernel,
        in_specs=[smem, smem] + [vmem] * 11,
        out_specs=anywhere,
        out_shape=jax.ShapeDtypeStruct(whole, jnp.float32),
        scratch_shapes=[buffer(*whole), pltpu.SemaphoreType.DMA((FIELDS,))],
        compiler_params=params,
        name="border",
    )(
        rotation,
        mortar_index,
        partial,
        lifter,
        near,
        far,
        from_low,
        from_high,
        from_below,
        from_above,
        metrics,
        cells,
        constant(mortar_columns()),
    )
    return out.reshape(1, 1, 1, FIELDS, NODES, ELEMS)


def solution(mesh):
    return jax.shard_map(
        local,
        mesh=mesh,
        in_specs=(
            P("side", "circ", "radial", None, None, None),
            P("side", "circ", "radial", None, None, None),
            P("side", "circ", "radial", None, None),
            P("side", "circ", "radial", None),
            P(),
            P("radial"),
        ),
        out_specs=P("side", "circ", "radial", None, None, None),
        check_vma=False,
    )
```

```python
import functools
import math

import jax
import jax.numpy as jnp
import numpy as np
from jax import lax
from jax.experimental import pallas as pl
from jax.experimental.pallas import tpu as pltpu
from jax.sharding import PartitionSpec as P

EL_C = 8
EL_R = 4
EL_A = 8
FRACS = 8
ELEMS = 256
NODES = 216
FIELDS = 5
STRIP = EL_R * EL_A

FLOW = (0.3, -0.2, 0.25)
WAVE = tuple(abs(u) + 1.0 for u in FLOW)
LIFT = 7.5
STEP = 0.02
WEIGHT = 0.25 * STEP

FACE = 40
IFACE = 48
FACES = 2 * FACE + 4 * IFACE
GROUP = 72
GROUPS = 3
CIRC_ROWS = 56
RADIAL_ROWS = 120
INTER_ROWS = 64
SLAB = 224
BLOCK = 144
SPREAD = 80
LIFTS = GROUPS * SLAB + BLOCK


def node_table():
    inner_point = math.sqrt(1.0 / 3.0 - 2.0 * math.sqrt(7.0) / 21.0)
    outer_point = math.sqrt(1.0 / 3.0 + 2.0 * math.sqrt(7.0) / 21.0)
    return np.array([-1.0, -outer_point, -inner_point, inner_point, outer_point, 1.0])


def derivative_table():
    abscissa = node_table()
    weights_bary = np.array(
        [np.prod([abscissa[i] - abscissa[m] for m in range(6) if m != i]) for i in range(6)]
    )
    matrix = np.zeros((6, 6))
    for i in range(6):
        for j in range(6):
            if i != j:
                matrix[i, j] = weights_bary[i] / (weights_bary[j] * (abscissa[i] - abscissa[j]))
        matrix[i, i] = -np.sum(matrix[i])
    return matrix


def basis_values(points):
    nodes_unit = (node_table() + 1.0) / 2.0
    values = np.ones((points.shape[0], 6))
    for j in range(6):
        for m in range(6):
            if m != j:
                values[:, j] = (
                    values[:, j] * (points - nodes_unit[m]) / (nodes_unit[j] - nodes_unit[m])
                )
    return values


def mortar_tables():
    nodes_unit = (node_table() + 1.0) / 2.0
    tables = np.zeros((4, FRACS, 6, 6))
    for k in range(FRACS):
        fraction = k / FRACS
        beyond = nodes_unit >= fraction
        tables[0, k] = np.where(beyond[:, None], basis_values(nodes_unit - fraction), 0.0)
        tables[1, k] = np.where(beyond[:, None], 0.0, basis_values(nodes_unit - fraction + 1.0))
        crossing = nodes_unit + fraction >= 1.0
        tables[2, k] = np.where(crossing[:, None], 0.0, basis_values(nodes_unit + fraction))
        tables[3, k] = np.where(crossing[:, None], basis_values(nodes_unit + fraction - 1.0), 0.0)
    return tables


def split_np(values):
    high = values.astype(jnp.bfloat16)
    low = (values - high.astype(np.float64)).astype(jnp.bfloat16)
    return high, low


def group_slots():
    slots = []
    for low in range(2):
        for other in range(6):
            row = 8 * low + other
            for end in range(2):
                slots.append((16 * end + row, 36 * low + 30 * end + other))
                slots.append((32 + 16 * end + row, 36 * low + 6 * other + 5 * end))
    return slots


def group_picker():
    table = np.zeros((64, 2 * GROUP))
    for row, node in group_slots():
        table[row, node] = 1.0
        table[row, GROUP + node] = 1.0
    return table


def node_tables():
    one = -derivative_table()
    one[0, 0] -= LIFT
    one[5, 5] += LIFT
    table = np.zeros((LIFTS + GROUPS * SPREAD, 3 * GROUP))

    def put(start, matrix):
        high, low = split_np(matrix)
        for k, values in enumerate((high, high, low)):
            table[start : start + matrix.shape[0], k * GROUP : (k + 1) * GROUP] = values

    circ = np.kron(one, np.eye(36))
    for g in range(GROUPS):
        put(g * SLAB, circ[:, g * GROUP : (g + 1) * GROUP])
        start = LIFTS + g * SPREAD
        places = [(node, row) for row, node in group_slots()]
        if g != 1:
            places += [(m + 18 * g, 64 + m) for m in range(36)]
        width = 64 if g == 1 else 64 + FACE
        for node, column in places:
            table[start + node, column] = 1.0
            table[start + node, width + column] = 1.0
    put(GROUPS * SLAB, np.kron(np.eye(2), np.kron(one, np.eye(6))))
    put(GROUPS * SLAB + GROUP, np.kron(np.eye(12), one))
    return table


def wave_columns():
    columns = np.zeros((NODES, 16))
    nodes = np.arange(NODES)
    for direction, stride in enumerate((36, 6, 1)):
        ends = nodes // stride % 6 % 5 == 0
        columns[:, direction] = -LIFT * WAVE[direction] * ends
        columns[:, 8 + direction] = columns[:, direction]
    return columns


def mortar_columns():
    tables = mortar_tables().reshape(4, FRACS, 36)
    table = np.zeros((80, 16))
    for k in range(FRACS):
        table[:36, k] = tables[2, k]
        table[40:76, k] = tables[3, k]
        table[:36, 8 + k] = tables[1, k]
        table[40:76, 8 + k] = tables[0, k]
    high = table.astype(jnp.bfloat16)
    rest = table - high.astype(np.float64)
    middle = rest.astype(jnp.bfloat16)
    low = (rest - middle.astype(np.float64)).astype(jnp.bfloat16)
    return np.concatenate([high, middle, low], axis=1)


def mm(a, b):
    return jnp.dot(a, b, preferred_element_type=jnp.float32)


def split(values):
    high = values.astype(jnp.bfloat16)
    low = (values - high.astype(jnp.float32)).astype(jnp.bfloat16)
    return high, low


def mm_split(values, table):
    rows = values.shape[0]
    high = values.astype(jnp.bfloat16).astype(jnp.float32)
    both = jnp.concatenate([high, values - high], axis=0).astype(jnp.bfloat16)
    product = mm(both, table)
    return product[:rows] + product[rows:]


def face_start(direction, end):
    return 2 * FACE * (direction > 0) + 2 * IFACE * (direction > 1) + face_rows(direction) * end


def face_rows(direction):
    return FACE if direction == 0 else IFACE


def lift(tables, terms):
    parts = []
    for g in range(GROUPS):
        rows = [face[16 * g : 16 * g + 16] for face in terms[2:]]
        if g != 1:
            rows.append(terms[g // 2])
        values = jnp.concatenate(rows, axis=0)
        high = values.astype(jnp.bfloat16).astype(jnp.float32)
        both = jnp.concatenate([high, values - high], axis=0).astype(jnp.bfloat16)
        start = LIFTS + g * SPREAD
        parts.append(mm(tables[start : start + SPREAD, : both.shape[0]], both)[:GROUP])
    return jnp.concatenate(parts, axis=0)


def hits(a, b):
    return (a == b).astype(jnp.float32).astype(jnp.bfloat16)


def cell_column(cell):
    rows = jnp.broadcast_to(cell.astype(jnp.float32), (8, ELEMS))
    return jnp.transpose(rows)[:, 0:1].astype(jnp.int32)


def border_cells(kind, index):
    if kind == "circ_low":
        return index
    if kind == "circ_high":
        return index + (EL_C - 1) * STRIP
    if kind == "radial_low":
        return (index // EL_A) * STRIP + index % EL_A
    if kind == "radial_high":
        return (index // EL_A) * STRIP + index % EL_A + (EL_R - 1) * EL_A
    return index * EL_A


def lanes_of(parts, width, rows):
    lane = lax.broadcasted_iota(jnp.int32, (rows, 128), 1) // width
    packed = parts[0:rows]
    for j in range(1, 128 // width):
        packed = jnp.where(lane == j, parts[j * rows : (j + 1) * rows], packed)
    return packed


def rows_of(packed, width, rows):
    lane = lax.broadcasted_iota(jnp.int32, (rows, 128), 1) // width
    return jnp.concatenate(
        [jnp.where(lane == j, packed, 0.0) for j in range(128 // width)], axis=0
    )


def start_all(pairs, sems):
    copies = [pltpu.make_async_copy(src, dst, sems.at[k]) for k, (src, dst) in enumerate(pairs)]
    for copy in copies:
        copy.start()
    return copies


def pack_kernel(
    current,
    cell_ref,
    metric,
    picker_hbm,
    operators_hbm,
    inter,
    circ_low,
    circ_high,
    radial_low,
    radial_high,
    pieces,
    traces,
    operators,
    cells,
    metrics,
    fields,
    picker,
    sems,
):
    side = lax.axis_index("side")
    copies = start_all(
        [(cell_ref, cells), (metric, metrics), (picker_hbm, picker)]
        + [(current.at[f], fields.at[f]) for f in range(FIELDS)]
        + [(operators_hbm, operators)],
        sems,
    )
    iota = lax.broadcasted_iota
    copies[0].wait()
    column = jnp.broadcast_to(cell_column(cells[...]), (ELEMS, 128))
    line = iota(jnp.int32, (1, 128), 1)
    jobs = (
        (circ_low, "circ_low", 0, FACE, 32, CIRC_ROWS),
        (circ_high, "circ_high", FACE, FACE, 32, CIRC_ROWS),
        (radial_low, "radial_low", face_start(1, 0), IFACE, 64, RADIAL_ROWS),
        (radial_high, "radial_high", face_start(1, 1), IFACE, 64, RADIAL_ROWS),
        (inter, "inter", face_start(2, 0), IFACE, 32, INTER_ROWS),
    )
    tables = []
    for out, kind, start, count, width, block in jobs:
        wanted = border_cells(kind, line % width)
        if kind == "inter":
            wanted = wanted + (EL_A - 1) * (1 - side)
        tables.append(hits(column, wanted))
    copies[1].wait()
    copies[2].wait()
    filler = jnp.zeros((FACE - 36, ELEMS), jnp.float32)
    for f in range(FIELDS):
        copies[3 + f].wait()
        traces[f, :FACE] = jnp.concatenate([fields[f, :36], filler], axis=0)
        traces[f, FACE : 2 * FACE] = jnp.concatenate([fields[f, 180:], filler], axis=0)
        for g in range(GROUPS):
            values = fields[f, g * GROUP : (g + 1) * GROUP]
            high = values.astype(jnp.bfloat16).astype(jnp.float32)
            both = jnp.concatenate([high, values - high], axis=0).astype(jnp.bfloat16)
            pieces[f, g] = both
            ends = mm(picker[...], both)
            for k in range(4):
                start = 2 * FACE + k * IFACE + 16 * g
                traces[f, start : start + 16] = ends[16 * k : 16 * k + 16]

    def rows(start, count, total):
        if start == face_start(2, 0):
            parts = [
                jnp.where(side == 0, traces[f, start + count :], traces[f, start : start + count])
                for f in range(FIELDS)
            ]
        else:
            parts = [traces[f, start : start + count] for f in range(FIELDS)]
        extra = total - FIELDS * count
        if extra:
            parts.append(jnp.zeros((extra, ELEMS), jnp.float32))
        return jnp.concatenate(parts, axis=0)

    for table, (out, kind, start, count, width, block) in zip(tables, jobs):
        values = mm_split(rows(start, count, block * (128 // width)), table)
        out[...] = lanes_of(values, width, block)
    copies[-1].wait()


def jump_terms(exterior, direction, sign, scale):
    first = (WAVE[direction] - sign * FLOW[direction]) * scale
    second = sign * scale
    terms = [first * e for e in exterior]
    terms[0] = terms[0] - second * exterior[1 + direction]
    terms[1 + direction] = terms[1 + direction] - second * exterior[0]
    return terms


def volume_kernel(
    pieces,
    traces,
    operators,
    cells,
    metrics,
    waves_hbm,
    base,
    result,
    waves,
    bases,
    sems,
):
    copies = start_all(
        [(waves_hbm, waves)] + [(base.at[f], bases.at[f]) for f in range(FIELDS)], sems
    )
    scale = [metrics[d] * WEIGHT for d in range(3)]
    cell = cells[...]
    cell_rows = jnp.broadcast_to(cell_column(cell), (ELEMS, ELEMS))
    place = (cell // STRIP, cell // EL_A % EL_R, cell % EL_A)
    length = (EL_C, EL_R, EL_A)
    stride = (STRIP, EL_A, 1)
    terms = [[] for _ in range(FIELDS)]
    for d in range(3):
        for end in range(2):
            if end == 0:
                wanted = jnp.where(place[d] == 0, -1, cell - stride[d])
            else:
                wanted = jnp.where(place[d] == length[d] - 1, -1, cell + stride[d])
            table = hits(cell_rows, wanted)
            count = face_rows(d)
            start = face_start(d, 1 - end)
            trace = [traces[f, start : start + count] for f in range(FIELDS)]
            outer = mm_split(jnp.concatenate(trace, axis=0), table)
            outer = [outer[f * count : (f + 1) * count] for f in range(FIELDS)]
            found = jump_terms(outer, d, 2.0 * end - 1.0, LIFT * scale[d])
            for f in range(FIELDS):
                terms[f].append(found[f])
    copies[0].wait()
    scaled = jnp.concatenate(scale, axis=0)
    filler = jnp.zeros((5, ELEMS), jnp.float32)
    scale_high = scaled.astype(jnp.bfloat16).astype(jnp.float32)
    scale_rows = jnp.concatenate([scaled, filler, scaled - scale_high, filler], axis=0)
    diagonal = 0.25 + mm(waves[...], scale_rows.astype(jnp.bfloat16))
    own = []
    for f in range(FIELDS):
        products = []
        field = []
        rights = []
        blank = jnp.zeros((ELEMS - 3 * GROUP, ELEMS), jnp.bfloat16)
        for g in range(GROUPS):
            both = pieces[f, g]
            right = jnp.concatenate([both, both[:GROUP], blank], axis=0)
            rights.append(right)
            both = both.astype(jnp.float32)
            field.append(both[:GROUP] + both[GROUP:])
        zero = jnp.zeros((SLAB, ELEMS - 3 * GROUP), jnp.bfloat16)
        left = [jnp.concatenate([operators[g * SLAB : (g + 1) * SLAB], zero], axis=1) for g in range(GROUPS)]
        rates = [mm(jnp.concatenate(left, axis=1), jnp.concatenate(rights, axis=0))[:NODES]]
        zero = jnp.zeros((BLOCK, ELEMS - 3 * GROUP), jnp.bfloat16)
        products = [mm(jnp.concatenate([operators[GROUPS * SLAB : LIFTS], zero], axis=1), r) for r in rights]
        for start in (0, GROUP):
            rates.append(jnp.concatenate([p[start : start + GROUP] for p in products], axis=0))
        total = diagonal * jnp.concatenate(field, axis=0) + lift(operators, terms[f])
        for d in range(3):
            total = total + (FLOW[d] * scale[d]) * rates[d]
        if f == 0:
            pressure = rates
        elif f < 4:
            total = total + scale[f - 1] * pressure[f - 1]
            own[0] = own[0] + scale[f - 1] * rates[f - 1]
        own.append(total)
    for f in range(FIELDS):
        copies[1 + f].wait()
        result[f] = own[f] + 0.75 * bases[f]


def border_kernel(
    rotation,
    mortar,
    partial,
    operators,
    near,
    far,
    from_low,
    from_high,
    from_below,
    from_above,
    metrics,
    cells,
    coefficients,
    out,
    result,
    out_sems,
):
    side = lax.axis_index("side")
    radial = lax.axis_index("radial")
    cell = cells[...]
    scale = [metrics[d] * (WEIGHT * LIFT) for d in range(3)]
    row = lax.broadcasted_iota(jnp.int32, (ELEMS, ELEMS), 0)
    row_of = {32: row % 32, 64: row % 64}
    circ_place = cell // STRIP
    radial_place = cell // EL_A % EL_R
    circ_index = cell % STRIP
    radial_index = circ_place * EL_A + cell % EL_A
    jobs = (
        (from_low, jnp.where(circ_place == 0, circ_index, -1), 0, 0, 32, CIRC_ROWS),
        (from_high, jnp.where(circ_place == EL_C - 1, circ_index, -1), 0, 1, 32, CIRC_ROWS),
        (from_below, jnp.where(radial_place == 0, radial_index, -1), 1, 0, 64, RADIAL_ROWS),
        (from_above, jnp.where(radial_place == EL_R - 1, radial_index, -1), 1, 1, 64, RADIAL_ROWS),
    )
    tables = [hits(row_of[width], index) for _, index, _, _, width, _ in jobs]
    remainder = rotation[0] % EL_C
    first = jnp.where(side == 0, remainder, EL_C - 1 - remainder)
    facing = cell % EL_A == (EL_A - 1) * (1 - side)
    pickers = []
    for later in range(2):
        at = circ_place + first + later
        index = at * EL_R + radial_place
        early_index = jnp.where(facing & (at < EL_C), index, -1)
        late_index = jnp.where(facing & (at >= EL_C), index - EL_C * EL_R, -1)
        pickers.append((hits(row_of[32], early_index), hits(row_of[32], late_index)))
    fraction = jnp.zeros_like(cell)
    for r in range(EL_R):
        fraction = jnp.where(radial_place == r, mortar[r], fraction)
    chosen = lax.broadcasted_iota(jnp.int32, (48, ELEMS), 0) % 16 == fraction + 8 * side
    weights = mm(coefficients[...], chosen.astype(jnp.float32).astype(jnp.bfloat16))

    def both(values):
        high = values.astype(jnp.bfloat16).astype(jnp.float32)
        return jnp.concatenate([high, values - high], axis=1).astype(jnp.bfloat16)

    terms = [[] for _ in range(FIELDS)]
    for table, (source, _, d, end, width, block) in zip(tables, jobs):
        outer = mm(both(rows_of(source[...], width, block)), table)
        count = face_rows(d)
        outer = [outer[f * count : (f + 1) * count] for f in range(FIELDS)]
        factor = scale[d]
        if d == 1:
            wall = 0 if end == 0 else 3
            factor = factor * jnp.where(radial == wall, 0.0, 1.0)
        found = jump_terms(outer, d, 2.0 * end - 1.0, factor)
        for f in range(FIELDS):
            terms[f].append(found[f])
    earlier = jnp.where(side == 0, near[...], far[...])
    later = jnp.where(side == 0, far[...], near[...])
    earlier_parts = both(rows_of(earlier, 32, INTER_ROWS))
    later_parts = both(rows_of(later, 32, INTER_ROWS))
    windows = [mm(earlier_parts, a) + mm(later_parts, b) for a, b in pickers]
    outer = []
    for f in range(FIELDS):
        blocks = []
        for i in range(6):
            total = None
            for later in range(2):
                for j in range(6):
                    at = 40 * later + 6 * i + j
                    start = f * IFACE + 8 * j
                    part = weights[at : at + 1] * windows[later][start : start + 8]
                    total = part if total is None else total + part
            blocks.append(total)
        outer.append(jnp.concatenate(blocks, axis=0))
    sign = jnp.where(side == 0, 1.0, -1.0)
    found = jump_terms(outer, 2, sign, scale[2])
    stores = []
    for f in range(FIELDS):
        terms[f].append(jnp.where(side == 1, found[f], 0.0))
        terms[f].append(jnp.where(side == 0, found[f], 0.0))
        result[f] = partial[f] + lift(operators, terms[f])
        stores.append(pltpu.make_async_copy(result.at[f], out.at[f], out_sems.at[f]))
        stores[f].start()
    for store in stores:
        store.wait()


def to_partner(shift):
    def send(block):
        pairs = []
        for k in range(32):
            other = (k + shift) % 32
            pairs += [(2 * k, 2 * other + 1), (2 * other + 1, 2 * k)]
        return lax.ppermute(block, ("circ", "side"), pairs)

    return send


def to_beside(block):
    pairs = []
    for k in range(32):
        pairs += [(2 * k, 2 * ((k - 1) % 32)), (2 * k + 1, 2 * ((k + 1) % 32) + 1)]
    return lax.ppermute(block, ("circ", "side"), pairs)


def ring(block, axis, step):
    count = lax.axis_size(axis)
    return lax.ppermute(block, axis, [(i, (i + step) % count) for i in range(count)])


def constant(values):
    return jnp.asarray(np.asarray(values), dtype=jnp.bfloat16)


def local(current, section_base, metric, slot_cell, rotation, mortar_index):
    current = current.reshape(FIELDS, NODES, ELEMS)
    section_base = section_base.reshape(FIELDS, NODES, ELEMS)
    metric = metric.reshape(3, 1, ELEMS)
    cell = slot_cell.reshape(1, ELEMS)
    params = pltpu.CompilerParams(vmem_limit_bytes=24 * 1024 * 1024)
    smem = pl.BlockSpec(memory_space=pltpu.SMEM)
    vmem = pl.BlockSpec(memory_space=pltpu.VMEM)
    anywhere = pl.BlockSpec(memory_space=pl.ANY)
    whole = (FIELDS, NODES, ELEMS)

    def buffer(*dims, kind=jnp.float32):
        return pltpu.VMEM(dims, kind)

    current, section_base, metric, cell = (
        pltpu.with_memory_space_constraint(x, pltpu.HBM)
        for x in (current, section_base, metric, cell)
    )
    tables = node_tables()
    picker = group_picker()
    packed = pl.pallas_call(
        pack_kernel,
        in_specs=[anywhere] * 5,
        out_specs=[vmem] * 10,
        out_shape=[
            buffer(INTER_ROWS, 128),
            buffer(CIRC_ROWS, 128),
            buffer(CIRC_ROWS, 128),
            buffer(RADIAL_ROWS, 128),
            buffer(RADIAL_ROWS, 128),
            buffer(FIELDS, GROUPS, 2 * GROUP, ELEMS, kind=jnp.bfloat16),
            buffer(FIELDS, FACES, ELEMS),
            buffer(*tables.shape, kind=jnp.bfloat16),
            buffer(1, ELEMS, kind=jnp.int32),
            buffer(3, 1, ELEMS),
        ],
        scratch_shapes=[
            buffer(*whole),
            buffer(*picker.shape, kind=jnp.bfloat16),
            pltpu.SemaphoreType.DMA((4 + FIELDS,)),
        ],
        compiler_params=params,
        name="pack",
    )(
        current,
        cell,
        metric,
        pltpu.with_memory_space_constraint(constant(picker), pltpu.HBM),
        pltpu.with_memory_space_constraint(constant(tables), pltpu.HBM),
    )
    inter, circ_low, circ_high, radial_low, radial_high = packed[:5]
    pieces, traces, operators, cells, metrics = packed[5:]
    from_low = ring(circ_high, "circ", 1)
    from_high = ring(circ_low, "circ", -1)
    from_below = ring(radial_high, "radial", 1)
    from_above = ring(radial_low, "radial", -1)
    near = lax.switch(
        jnp.right_shift(rotation[0], 3), [to_partner(k) for k in range(32)], inter
    )
    far = to_beside(near)
    metrics, near = lax.optimization_barrier((metrics, near))
    partial = pl.pallas_call(
        volume_kernel,
        in_specs=[vmem] * 5 + [anywhere] * 2,
        out_specs=vmem,
        out_shape=buffer(*whole),
        scratch_shapes=[
            buffer(NODES, 16, kind=jnp.bfloat16),
            buffer(*whole),
            pltpu.SemaphoreType.DMA((1 + FIELDS,)),
        ],
        compiler_params=params,
        cost_estimate=pl.CostEstimate(
            flops=4 * 10**9, bytes_accessed=4 * 10**6, transcendentals=0
        ),
        name="volume",
    )(
        pieces,
        traces,
        operators,
        cells,
        metrics,
        pltpu.with_memory_space_constraint(constant(wave_columns()), pltpu.HBM),
        section_base,
    )
    out = pl.pallas_call(
        border_kernel,
        in_specs=[smem, smem] + [vmem] * 11,
        out_specs=anywhere,
        out_shape=jax.ShapeDtypeStruct(whole, jnp.float32),
        scratch_shapes=[buffer(*whole), pltpu.SemaphoreType.DMA((FIELDS,))],
        compiler_params=params,
        name="border",
    )(
        rotation,
        mortar_index,
        partial,
        operators,
        near,
        far,
        from_low,
        from_high,
        from_below,
        from_above,
        metrics,
        cells,
        constant(mortar_columns()),
    )
    return out.reshape(1, 1, 1, FIELDS, NODES, ELEMS)


def solution(mesh):
    return jax.shard_map(
        local,
        mesh=mesh,
        in_specs=(
            P("side", "circ", "radial", None, None, None),
            P("side", "circ", "radial", None, None, None),
            P("side", "circ", "radial", None, None),
            P("side", "circ", "radial", None),
            P(),
            P("radial"),
        ),
        out_specs=P("side", "circ", "radial", None, None, None),
        check_vma=False,
    )
```

```python
import functools
import math

import jax
import jax.numpy as jnp
import numpy as np
from jax import lax
from jax.experimental import pallas as pl
from jax.experimental.pallas import tpu as pltpu
from jax.sharding import PartitionSpec as P

EL_C = 8
EL_R = 4
EL_A = 8
FRACS = 8
ELEMS = 256
NODES = 216
FIELDS = 5
STRIP = EL_R * EL_A

FLOW = (0.3, -0.2, 0.25)
WAVE = tuple(abs(u) + 1.0 for u in FLOW)
LIFT = 7.5
STEP = 0.02
WEIGHT = 0.25 * STEP

FACE = 40
IFACE = 48
FACES = 2 * FACE + 4 * IFACE
GROUP = 72
GROUPS = 3
CIRC_ROWS = 56
RADIAL_ROWS = 120
INTER_ROWS = 64
SLAB = 224
BLOCK = 144
SPREAD = 80
LIFTS = GROUPS * SLAB + BLOCK


def node_table():
    inner_point = math.sqrt(1.0 / 3.0 - 2.0 * math.sqrt(7.0) / 21.0)
    outer_point = math.sqrt(1.0 / 3.0 + 2.0 * math.sqrt(7.0) / 21.0)
    return np.array([-1.0, -outer_point, -inner_point, inner_point, outer_point, 1.0])


def derivative_table():
    abscissa = node_table()
    weights_bary = np.array(
        [np.prod([abscissa[i] - abscissa[m] for m in range(6) if m != i]) for i in range(6)]
    )
    matrix = np.zeros((6, 6))
    for i in range(6):
        for j in range(6):
            if i != j:
                matrix[i, j] = weights_bary[i] / (weights_bary[j] * (abscissa[i] - abscissa[j]))
        matrix[i, i] = -np.sum(matrix[i])
    return matrix


def basis_values(points):
    nodes_unit = (node_table() + 1.0) / 2.0
    values = np.ones((points.shape[0], 6))
    for j in range(6):
        for m in range(6):
            if m != j:
                values[:, j] = (
                    values[:, j] * (points - nodes_unit[m]) / (nodes_unit[j] - nodes_unit[m])
                )
    return values


def mortar_tables():
    nodes_unit = (node_table() + 1.0) / 2.0
    tables = np.zeros((4, FRACS, 6, 6))
    for k in range(FRACS):
        fraction = k / FRACS
        beyond = nodes_unit >= fraction
        tables[0, k] = np.where(beyond[:, None], basis_values(nodes_unit - fraction), 0.0)
        tables[1, k] = np.where(beyond[:, None], 0.0, basis_values(nodes_unit - fraction + 1.0))
        crossing = nodes_unit + fraction >= 1.0
        tables[2, k] = np.where(crossing[:, None], 0.0, basis_values(nodes_unit + fraction))
        tables[3, k] = np.where(crossing[:, None], basis_values(nodes_unit + fraction - 1.0), 0.0)
    return tables


def split_np(values):
    high = values.astype(jnp.bfloat16)
    low = (values - high.astype(np.float64)).astype(jnp.bfloat16)
    return high, low


def group_slots():
    slots = []
    for low in range(2):
        for other in range(6):
            row = 8 * low + other
            for end in range(2):
                slots.append((16 * end + row, 36 * low + 30 * end + other))
                slots.append((32 + 16 * end + row, 36 * low + 6 * other + 5 * end))
    return slots


def group_picker():
    table = np.zeros((64, 2 * GROUP))
    for row, node in group_slots():
        table[row, node] = 1.0
        table[row, GROUP + node] = 1.0
    return table


def node_tables():
    one = -derivative_table()
    one[0, 0] -= LIFT
    one[5, 5] += LIFT
    table = np.zeros((LIFTS + GROUPS * SPREAD, 3 * GROUP))

    def put(start, matrix):
        high, low = split_np(matrix)
        for k, values in enumerate((high, high, low)):
            table[start : start + matrix.shape[0], k * GROUP : (k + 1) * GROUP] = values

    circ = np.kron(one, np.eye(36))
    for g in range(GROUPS):
        put(g * SLAB, circ[:, g * GROUP : (g + 1) * GROUP])
        start = LIFTS + g * SPREAD
        places = [(node, row) for row, node in group_slots()]
        if g != 1:
            places += [(m + 18 * g, 64 + m) for m in range(36)]
        width = 64 if g == 1 else 64 + FACE
        for node, column in places:
            table[start + node, column] = 1.0
            table[start + node, width + column] = 1.0
    put(GROUPS * SLAB, np.kron(np.eye(2), np.kron(one, np.eye(6))))
    put(GROUPS * SLAB + GROUP, np.kron(np.eye(12), one))
    return table


def wave_columns():
    columns = np.zeros((NODES, 16))
    nodes = np.arange(NODES)
    for direction, stride in enumerate((36, 6, 1)):
        ends = nodes // stride % 6 % 5 == 0
        columns[:, direction] = -LIFT * WAVE[direction] * ends
        columns[:, 8 + direction] = columns[:, direction]
    return columns


def mortar_columns():
    tables = mortar_tables().reshape(4, FRACS, 36)
    table = np.zeros((80, 16))
    for k in range(FRACS):
        table[:36, k] = tables[2, k]
        table[40:76, k] = tables[3, k]
        table[:36, 8 + k] = tables[1, k]
        table[40:76, 8 + k] = tables[0, k]
    high = table.astype(jnp.bfloat16)
    rest = table - high.astype(np.float64)
    middle = rest.astype(jnp.bfloat16)
    low = (rest - middle.astype(np.float64)).astype(jnp.bfloat16)
    return np.concatenate([high, middle, low], axis=1)


def mm(a, b):
    return jnp.dot(a, b, preferred_element_type=jnp.float32)


def split(values):
    high = values.astype(jnp.bfloat16)
    low = (values - high.astype(jnp.float32)).astype(jnp.bfloat16)
    return high, low


def mm_split(values, table):
    rows = values.shape[0]
    high = values.astype(jnp.bfloat16).astype(jnp.float32)
    both = jnp.concatenate([high, values - high], axis=0).astype(jnp.bfloat16)
    product = mm(both, table)
    return product[:rows] + product[rows:]


def face_start(direction, end):
    return 2 * FACE * (direction > 0) + 2 * IFACE * (direction > 1) + face_rows(direction) * end


def face_rows(direction):
    return FACE if direction == 0 else IFACE


def lift(tables, terms):
    parts = []
    for g in range(GROUPS):
        rows = [face[16 * g : 16 * g + 16] for face in terms[2:]]
        if g != 1:
            rows.append(terms[g // 2])
        values = jnp.concatenate(rows, axis=0)
        high = values.astype(jnp.bfloat16).astype(jnp.float32)
        both = jnp.concatenate([high, values - high], axis=0).astype(jnp.bfloat16)
        start = LIFTS + g * SPREAD
        parts.append(mm(tables[start : start + SPREAD, : both.shape[0]], both)[:GROUP])
    return jnp.concatenate(parts, axis=0)


def hits(a, b):
    return (a == b).astype(jnp.float32).astype(jnp.bfloat16)


def cell_column(cell):
    rows = jnp.broadcast_to(cell.astype(jnp.float32), (8, ELEMS))
    return jnp.transpose(rows)[:, 0:1].astype(jnp.int32)


def border_cells(kind, index):
    if kind == "circ_low":
        return index
    if kind == "circ_high":
        return index + (EL_C - 1) * STRIP
    if kind == "radial_low":
        return (index // EL_A) * STRIP + index % EL_A
    if kind == "radial_high":
        return (index // EL_A) * STRIP + index % EL_A + (EL_R - 1) * EL_A
    return index * EL_A


def lanes_of(parts, width, rows):
    lane = lax.broadcasted_iota(jnp.int32, (rows, 128), 1) // width
    packed = parts[0:rows]
    for j in range(1, 128 // width):
        packed = jnp.where(lane == j, parts[j * rows : (j + 1) * rows], packed)
    return packed


def rows_of(packed, width, rows):
    lane = lax.broadcasted_iota(jnp.int32, (rows, 128), 1) // width
    return jnp.concatenate(
        [jnp.where(lane == j, packed, 0.0) for j in range(128 // width)], axis=0
    )


def start_all(pairs, sems):
    copies = [pltpu.make_async_copy(src, dst, sems.at[k]) for k, (src, dst) in enumerate(pairs)]
    for copy in copies:
        copy.start()
    return copies


def pack_kernel(
    current,
    cell_ref,
    metric,
    picker_hbm,
    operators_hbm,
    inter,
    circ_low,
    circ_high,
    radial_low,
    radial_high,
    pieces,
    traces,
    operators,
    cells,
    metrics,
    fields,
    picker,
    sems,
):
    side = lax.axis_index("side")
    copies = start_all(
        [(cell_ref, cells), (metric, metrics), (picker_hbm, picker)]
        + [(current.at[f], fields.at[f]) for f in range(FIELDS)]
        + [(operators_hbm, operators)],
        sems,
    )
    iota = lax.broadcasted_iota
    copies[0].wait()
    column = jnp.broadcast_to(cell_column(cells[...]), (ELEMS, 128))
    line = iota(jnp.int32, (1, 128), 1)
    jobs = (
        (circ_low, "circ_low", 0, FACE, 32, CIRC_ROWS),
        (circ_high, "circ_high", FACE, FACE, 32, CIRC_ROWS),
        (radial_low, "radial_low", face_start(1, 0), IFACE, 64, RADIAL_ROWS),
        (radial_high, "radial_high", face_start(1, 1), IFACE, 64, RADIAL_ROWS),
        (inter, "inter", face_start(2, 0), IFACE, 32, INTER_ROWS),
    )
    tables = []
    for out, kind, start, count, width, block in jobs:
        wanted = border_cells(kind, line % width)
        if kind == "inter":
            wanted = wanted + (EL_A - 1) * (1 - side)
        tables.append(hits(column, wanted))
    copies[1].wait()
    copies[2].wait()
    filler = jnp.zeros((FACE - 36, ELEMS), jnp.float32)
    for f in range(FIELDS):
        copies[3 + f].wait()
        traces[f, :FACE] = jnp.concatenate([fields[f, :36], filler], axis=0)
        traces[f, FACE : 2 * FACE] = jnp.concatenate([fields[f, 180:], filler], axis=0)
        for g in range(GROUPS):
            values = fields[f, g * GROUP : (g + 1) * GROUP]
            high = values.astype(jnp.bfloat16).astype(jnp.float32)
            both = jnp.concatenate([high, values - high], axis=0).astype(jnp.bfloat16)
            pieces[f, g] = both
            ends = mm(picker[...], both)
            for k in range(4):
                start = 2 * FACE + k * IFACE + 16 * g
                traces[f, start : start + 16] = ends[16 * k : 16 * k + 16]

    def rows(start, count, total):
        if start == face_start(2, 0):
            parts = [
                jnp.where(side == 0, traces[f, start + count :], traces[f, start : start + count])
                for f in range(FIELDS)
            ]
        else:
            parts = [traces[f, start : start + count] for f in range(FIELDS)]
        extra = total - FIELDS * count
        if extra:
            parts.append(jnp.zeros((extra, ELEMS), jnp.float32))
        return jnp.concatenate(parts, axis=0)

    for table, (out, kind, start, count, width, block) in zip(tables, jobs):
        values = mm_split(rows(start, count, block * (128 // width)), table)
        out[...] = lanes_of(values, width, block)
    copies[-1].wait()


def jump_terms(exterior, direction, sign, scale):
    first = (WAVE[direction] - sign * FLOW[direction]) * scale
    second = sign * scale
    terms = [first * e for e in exterior]
    terms[0] = terms[0] - second * exterior[1 + direction]
    terms[1 + direction] = terms[1 + direction] - second * exterior[0]
    return terms


def volume_kernel(
    pieces,
    traces,
    operators,
    cells,
    metrics,
    waves_hbm,
    base,
    near_hbm,
    result,
    near,
    waves,
    bases,
    sems,
):
    copies = start_all(
        [(waves_hbm, waves)]
        + [(base.at[f], bases.at[f]) for f in range(FIELDS)]
        + [(near_hbm, near)],
        sems,
    )
    scale = [metrics[d] * WEIGHT for d in range(3)]
    cell = cells[...]
    cell_rows = jnp.broadcast_to(cell_column(cell), (ELEMS, ELEMS))
    place = (cell // STRIP, cell // EL_A % EL_R, cell % EL_A)
    length = (EL_C, EL_R, EL_A)
    stride = (STRIP, EL_A, 1)
    terms = [[] for _ in range(FIELDS)]
    for d in range(3):
        for end in range(2):
            if end == 0:
                wanted = jnp.where(place[d] == 0, -1, cell - stride[d])
            else:
                wanted = jnp.where(place[d] == length[d] - 1, -1, cell + stride[d])
            table = hits(cell_rows, wanted)
            count = face_rows(d)
            start = face_start(d, 1 - end)
            trace = [traces[f, start : start + count] for f in range(FIELDS)]
            outer = mm_split(jnp.concatenate(trace, axis=0), table)
            outer = [outer[f * count : (f + 1) * count] for f in range(FIELDS)]
            found = jump_terms(outer, d, 2.0 * end - 1.0, LIFT * scale[d])
            for f in range(FIELDS):
                terms[f].append(found[f])
    copies[0].wait()
    scaled = jnp.concatenate(scale, axis=0)
    filler = jnp.zeros((5, ELEMS), jnp.float32)
    scale_high = scaled.astype(jnp.bfloat16).astype(jnp.float32)
    scale_rows = jnp.concatenate([scaled, filler, scaled - scale_high, filler], axis=0)
    diagonal = 0.25 + mm(waves[...], scale_rows.astype(jnp.bfloat16))
    own = []
    for f in range(FIELDS):
        products = []
        field = []
        rights = []
        blank = jnp.zeros((ELEMS - 3 * GROUP, ELEMS), jnp.bfloat16)
        for g in range(GROUPS):
            both = pieces[f, g]
            right = jnp.concatenate([both, both[:GROUP], blank], axis=0)
            rights.append(right)
            both = both.astype(jnp.float32)
            field.append(both[:GROUP] + both[GROUP:])
        zero = jnp.zeros((SLAB, ELEMS - 3 * GROUP), jnp.bfloat16)
        left = [jnp.concatenate([operators[g * SLAB : (g + 1) * SLAB], zero], axis=1) for g in range(GROUPS)]
        rates = [mm(jnp.concatenate(left, axis=1), jnp.concatenate(rights, axis=0))[:NODES]]
        zero = jnp.zeros((BLOCK, ELEMS - 3 * GROUP), jnp.bfloat16)
        products = [mm(jnp.concatenate([operators[GROUPS * SLAB : LIFTS], zero], axis=1), r) for r in rights]
        for start in (0, GROUP):
            rates.append(jnp.concatenate([p[start : start + GROUP] for p in products], axis=0))
        total = diagonal * jnp.concatenate(field, axis=0) + lift(operators, terms[f])
        for d in range(3):
            total = total + (FLOW[d] * scale[d]) * rates[d]
        if f == 0:
            pressure = rates
        elif f < 4:
            total = total + scale[f - 1] * pressure[f - 1]
            own[0] = own[0] + scale[f - 1] * rates[f - 1]
        own.append(total)
    for f in range(FIELDS):
        copies[1 + f].wait()
        result[f] = own[f] + 0.75 * bases[f]
    copies[-1].wait()


def border_kernel(
    rotation,
    mortar,
    partial,
    operators,
    near,
    far,
    from_low,
    from_high,
    from_below,
    from_above,
    metrics,
    cells,
    coefficients,
    out,
    result,
    out_sems,
):
    side = lax.axis_index("side")
    radial = lax.axis_index("radial")
    cell = cells[...]
    scale = [metrics[d] * (WEIGHT * LIFT) for d in range(3)]
    row = lax.broadcasted_iota(jnp.int32, (ELEMS, ELEMS), 0)
    row_of = {32: row % 32, 64: row % 64}
    circ_place = cell // STRIP
    radial_place = cell // EL_A % EL_R
    circ_index = cell % STRIP
    radial_index = circ_place * EL_A + cell % EL_A
    jobs = (
        (from_low, jnp.where(circ_place == 0, circ_index, -1), 0, 0, 32, CIRC_ROWS),
        (from_high, jnp.where(circ_place == EL_C - 1, circ_index, -1), 0, 1, 32, CIRC_ROWS),
        (from_below, jnp.where(radial_place == 0, radial_index, -1), 1, 0, 64, RADIAL_ROWS),
        (from_above, jnp.where(radial_place == EL_R - 1, radial_index, -1), 1, 1, 64, RADIAL_ROWS),
    )
    tables = [hits(row_of[width], index) for _, index, _, _, width, _ in jobs]
    remainder = rotation[0] % EL_C
    first = jnp.where(side == 0, remainder, EL_C - 1 - remainder)
    facing = cell % EL_A == (EL_A - 1) * (1 - side)
    pickers = []
    for later in range(2):
        at = circ_place + first + later
        index = at * EL_R + radial_place
        early_index = jnp.where(facing & (at < EL_C), index, -1)
        late_index = jnp.where(facing & (at >= EL_C), index - EL_C * EL_R, -1)
        pickers.append((hits(row_of[32], early_index), hits(row_of[32], late_index)))
    fraction = jnp.zeros_like(cell)
    for r in range(EL_R):
        fraction = jnp.where(radial_place == r, mortar[r], fraction)
    chosen = lax.broadcasted_iota(jnp.int32, (48, ELEMS), 0) % 16 == fraction + 8 * side
    weights = mm(coefficients[...], chosen.astype(jnp.float32).astype(jnp.bfloat16))

    def both(values):
        high = values.astype(jnp.bfloat16).astype(jnp.float32)
        return jnp.concatenate([high, values - high], axis=1).astype(jnp.bfloat16)

    terms = [[] for _ in range(FIELDS)]
    for table, (source, _, d, end, width, block) in zip(tables, jobs):
        outer = mm(both(rows_of(source[...], width, block)), table)
        count = face_rows(d)
        outer = [outer[f * count : (f + 1) * count] for f in range(FIELDS)]
        factor = scale[d]
        if d == 1:
            wall = 0 if end == 0 else 3
            factor = factor * jnp.where(radial == wall, 0.0, 1.0)
        found = jump_terms(outer, d, 2.0 * end - 1.0, factor)
        for f in range(FIELDS):
            terms[f].append(found[f])
    earlier = jnp.where(side == 0, near[...], far[...])
    later = jnp.where(side == 0, far[...], near[...])
    earlier_parts = both(rows_of(earlier, 32, INTER_ROWS))
    later_parts = both(rows_of(later, 32, INTER_ROWS))
    windows = [mm(earlier_parts, a) + mm(later_parts, b) for a, b in pickers]
    outer = []
    for f in range(FIELDS):
        blocks = []
        for i in range(6):
            total = None
            for later in range(2):
                for j in range(6):
                    at = 40 * later + 6 * i + j
                    start = f * IFACE + 8 * j
                    part = weights[at : at + 1] * windows[later][start : start + 8]
                    total = part if total is None else total + part
            blocks.append(total)
        outer.append(jnp.concatenate(blocks, axis=0))
    sign = jnp.where(side == 0, 1.0, -1.0)
    found = jump_terms(outer, 2, sign, scale[2])
    stores = []
    for f in range(FIELDS):
        terms[f].append(jnp.where(side == 1, found[f], 0.0))
        terms[f].append(jnp.where(side == 0, found[f], 0.0))
        result[f] = partial[f] + lift(operators, terms[f])
        stores.append(pltpu.make_async_copy(result.at[f], out.at[f], out_sems.at[f]))
        stores[f].start()
    for store in stores:
        store.wait()


def to_partner(shift):
    def send(block):
        pairs = []
        for k in range(32):
            other = (k + shift) % 32
            pairs += [(2 * k, 2 * other + 1), (2 * other + 1, 2 * k)]
        return lax.ppermute(block, ("circ", "side"), pairs)

    return send


def to_beside(block):
    pairs = []
    for k in range(32):
        pairs += [(2 * k, 2 * ((k - 1) % 32)), (2 * k + 1, 2 * ((k + 1) % 32) + 1)]
    return lax.ppermute(block, ("circ", "side"), pairs)


def ring(block, axis, step):
    count = lax.axis_size(axis)
    return lax.ppermute(block, axis, [(i, (i + step) % count) for i in range(count)])


def constant(values):
    return jnp.asarray(np.asarray(values), dtype=jnp.bfloat16)


def local(current, section_base, metric, slot_cell, rotation, mortar_index):
    current = current.reshape(FIELDS, NODES, ELEMS)
    section_base = section_base.reshape(FIELDS, NODES, ELEMS)
    metric = metric.reshape(3, 1, ELEMS)
    cell = slot_cell.reshape(1, ELEMS)
    params = pltpu.CompilerParams(vmem_limit_bytes=24 * 1024 * 1024)
    smem = pl.BlockSpec(memory_space=pltpu.SMEM)
    vmem = pl.BlockSpec(memory_space=pltpu.VMEM)
    anywhere = pl.BlockSpec(memory_space=pl.ANY)
    whole = (FIELDS, NODES, ELEMS)

    def buffer(*dims, kind=jnp.float32):
        return pltpu.VMEM(dims, kind)

    current, section_base, metric, cell = (
        pltpu.with_memory_space_constraint(x, pltpu.HBM)
        for x in (current, section_base, metric, cell)
    )
    tables = node_tables()
    picker = group_picker()
    packed = pl.pallas_call(
        pack_kernel,
        in_specs=[anywhere] * 5,
        out_specs=[vmem] * 10,
        out_shape=[
            buffer(INTER_ROWS, 128),
            buffer(CIRC_ROWS, 128),
            buffer(CIRC_ROWS, 128),
            buffer(RADIAL_ROWS, 128),
            buffer(RADIAL_ROWS, 128),
            buffer(FIELDS, GROUPS, 2 * GROUP, ELEMS, kind=jnp.bfloat16),
            buffer(FIELDS, FACES, ELEMS),
            buffer(*tables.shape, kind=jnp.bfloat16),
            buffer(1, ELEMS, kind=jnp.int32),
            buffer(3, 1, ELEMS),
        ],
        scratch_shapes=[
            buffer(*whole),
            buffer(*picker.shape, kind=jnp.bfloat16),
            pltpu.SemaphoreType.DMA((4 + FIELDS,)),
        ],
        compiler_params=params,
        name="pack",
    )(
        current,
        cell,
        metric,
        pltpu.with_memory_space_constraint(constant(picker), pltpu.HBM),
        pltpu.with_memory_space_constraint(constant(tables), pltpu.HBM),
    )
    inter, circ_low, circ_high, radial_low, radial_high = packed[:5]
    pieces, traces, operators, cells, metrics = packed[5:]
    from_low = ring(circ_high, "circ", 1)
    from_high = ring(circ_low, "circ", -1)
    from_below = ring(radial_high, "radial", 1)
    from_above = ring(radial_low, "radial", -1)
    near = lax.switch(
        jnp.right_shift(rotation[0], 3), [to_partner(k) for k in range(32)], inter
    )
    far = to_beside(near)
    metrics, near = lax.optimization_barrier((metrics, near))
    partial, near = pl.pallas_call(
        volume_kernel,
        in_specs=[vmem] * 5 + [anywhere] * 3,
        out_specs=[vmem] * 2,
        out_shape=[buffer(*whole), buffer(INTER_ROWS, 128)],
        scratch_shapes=[
            buffer(NODES, 16, kind=jnp.bfloat16),
            buffer(*whole),
            pltpu.SemaphoreType.DMA((2 + FIELDS,)),
        ],
        compiler_params=params,
        cost_estimate=pl.CostEstimate(
            flops=4 * 10**9, bytes_accessed=4 * 10**6, transcendentals=0
        ),
        name="volume",
    )(
        pieces,
        traces,
        operators,
        cells,
        metrics,
        pltpu.with_memory_space_constraint(constant(wave_columns()), pltpu.HBM),
        section_base,
        near,
    )
    out = pl.pallas_call(
        border_kernel,
        in_specs=[smem, smem] + [vmem] * 11,
        out_specs=anywhere,
        out_shape=jax.ShapeDtypeStruct(whole, jnp.float32),
        scratch_shapes=[buffer(*whole), pltpu.SemaphoreType.DMA((FIELDS,))],
        compiler_params=params,
        name="border",
    )(
        rotation,
        mortar_index,
        partial,
        operators,
        near,
        far,
        from_low,
        from_high,
        from_below,
        from_above,
        metrics,
        cells,
        constant(mortar_columns()),
    )
    return out.reshape(1, 1, 1, FIELDS, NODES, ELEMS)


def solution(mesh):
    return jax.shard_map(
        local,
        mesh=mesh,
        in_specs=(
            P("side", "circ", "radial", None, None, None),
            P("side", "circ", "radial", None, None, None),
            P("side", "circ", "radial", None, None),
            P("side", "circ", "radial", None),
            P(),
            P("radial"),
        ),
        out_specs=P("side", "circ", "radial", None, None, None),
        check_vma=False,
    )
```

```python
import functools
import math

import jax
import jax.numpy as jnp
import numpy as np
from jax import lax
from jax.experimental import pallas as pl
from jax.experimental.pallas import tpu as pltpu
from jax.sharding import PartitionSpec as P

EL_C = 8
EL_R = 4
EL_A = 8
FRACS = 8
ELEMS = 256
NODES = 216
FIELDS = 5
STRIP = EL_R * EL_A

FLOW = (0.3, -0.2, 0.25)
WAVE = tuple(abs(u) + 1.0 for u in FLOW)
LIFT = 7.5
STEP = 0.02
WEIGHT = 0.25 * STEP

FACE = 40
IFACE = 48
FACES = 2 * FACE + 4 * IFACE
GROUP = 72
GROUPS = 3
CIRC_ROWS = 56
RADIAL_ROWS = 120
INTER_ROWS = 64
SLAB = 224
BLOCK = 144
SPREAD = 80
LIFTS = GROUPS * SLAB + BLOCK


def node_table():
    inner_point = math.sqrt(1.0 / 3.0 - 2.0 * math.sqrt(7.0) / 21.0)
    outer_point = math.sqrt(1.0 / 3.0 + 2.0 * math.sqrt(7.0) / 21.0)
    return np.array([-1.0, -outer_point, -inner_point, inner_point, outer_point, 1.0])


def derivative_table():
    abscissa = node_table()
    weights_bary = np.array(
        [np.prod([abscissa[i] - abscissa[m] for m in range(6) if m != i]) for i in range(6)]
    )
    matrix = np.zeros((6, 6))
    for i in range(6):
        for j in range(6):
            if i != j:
                matrix[i, j] = weights_bary[i] / (weights_bary[j] * (abscissa[i] - abscissa[j]))
        matrix[i, i] = -np.sum(matrix[i])
    return matrix


def basis_values(points):
    nodes_unit = (node_table() + 1.0) / 2.0
    values = np.ones((points.shape[0], 6))
    for j in range(6):
        for m in range(6):
            if m != j:
                values[:, j] = (
                    values[:, j] * (points - nodes_unit[m]) / (nodes_unit[j] - nodes_unit[m])
                )
    return values


def mortar_tables():
    nodes_unit = (node_table() + 1.0) / 2.0
    tables = np.zeros((4, FRACS, 6, 6))
    for k in range(FRACS):
        fraction = k / FRACS
        beyond = nodes_unit >= fraction
        tables[0, k] = np.where(beyond[:, None], basis_values(nodes_unit - fraction), 0.0)
        tables[1, k] = np.where(beyond[:, None], 0.0, basis_values(nodes_unit - fraction + 1.0))
        crossing = nodes_unit + fraction >= 1.0
        tables[2, k] = np.where(crossing[:, None], 0.0, basis_values(nodes_unit + fraction))
        tables[3, k] = np.where(crossing[:, None], basis_values(nodes_unit + fraction - 1.0), 0.0)
    return tables


def split_np(values):
    high = values.astype(jnp.bfloat16)
    low = (values - high.astype(np.float64)).astype(jnp.bfloat16)
    return high, low


def group_slots():
    slots = []
    for low in range(2):
        for other in range(6):
            row = 8 * low + other
            for end in range(2):
                slots.append((16 * end + row, 36 * low + 30 * end + other))
                slots.append((32 + 16 * end + row, 36 * low + 6 * other + 5 * end))
    return slots


def group_picker():
    table = np.zeros((64, 2 * GROUP))
    for row, node in group_slots():
        table[row, node] = 1.0
        table[row, GROUP + node] = 1.0
    return table


def node_tables():
    one = -derivative_table()
    one[0, 0] -= LIFT
    one[5, 5] += LIFT
    table = np.zeros((LIFTS + GROUPS * SPREAD, 3 * GROUP))

    def put(start, matrix):
        high, low = split_np(matrix)
        for k, values in enumerate((high, high, low)):
            table[start : start + matrix.shape[0], k * GROUP : (k + 1) * GROUP] = values

    circ = np.kron(one, np.eye(36))
    for g in range(GROUPS):
        put(g * SLAB, circ[:, g * GROUP : (g + 1) * GROUP])
        start = LIFTS + g * SPREAD
        places = [(node, row) for row, node in group_slots()]
        if g != 1:
            places += [(m + 18 * g, 64 + m) for m in range(36)]
        width = 64 if g == 1 else 64 + FACE
        for node, column in places:
            table[start + node, column] = 1.0
            table[start + node, width + column] = 1.0
    put(GROUPS * SLAB, np.kron(np.eye(2), np.kron(one, np.eye(6))))
    put(GROUPS * SLAB + GROUP, np.kron(np.eye(12), one))
    return table


def wave_columns():
    columns = np.zeros((NODES, 16))
    nodes = np.arange(NODES)
    for direction, stride in enumerate((36, 6, 1)):
        ends = nodes // stride % 6 % 5 == 0
        columns[:, direction] = -LIFT * WAVE[direction] * ends
        columns[:, 8 + direction] = columns[:, direction]
    return columns


def mortar_columns():
    tables = mortar_tables().reshape(4, FRACS, 36)
    table = np.zeros((80, 16))
    for k in range(FRACS):
        table[:36, k] = tables[2, k]
        table[40:76, k] = tables[3, k]
        table[:36, 8 + k] = tables[1, k]
        table[40:76, 8 + k] = tables[0, k]
    high = table.astype(jnp.bfloat16)
    rest = table - high.astype(np.float64)
    middle = rest.astype(jnp.bfloat16)
    low = (rest - middle.astype(np.float64)).astype(jnp.bfloat16)
    return np.concatenate([high, middle, low], axis=1)


def mm(a, b):
    return jnp.dot(a, b, preferred_element_type=jnp.float32)


def split(values):
    high = values.astype(jnp.bfloat16)
    low = (values - high.astype(jnp.float32)).astype(jnp.bfloat16)
    return high, low


def mm_split(values, table):
    rows = values.shape[0]
    high = values.astype(jnp.bfloat16).astype(jnp.float32)
    both = jnp.concatenate([high, values - high], axis=0).astype(jnp.bfloat16)
    product = mm(both, table)
    return product[:rows] + product[rows:]


def face_start(direction, end):
    return 2 * FACE * (direction > 0) + 2 * IFACE * (direction > 1) + face_rows(direction) * end


def face_rows(direction):
    return FACE if direction == 0 else IFACE


def lift(tables, terms):
    parts = []
    for g in range(GROUPS):
        rows = [face[16 * g : 16 * g + 16] for face in terms[2:]]
        if g != 1:
            rows.append(terms[g // 2])
        values = jnp.concatenate(rows, axis=0)
        high = values.astype(jnp.bfloat16).astype(jnp.float32)
        both = jnp.concatenate([high, values - high], axis=0).astype(jnp.bfloat16)
        start = LIFTS + g * SPREAD
        parts.append(mm(tables[start : start + SPREAD, : both.shape[0]], both)[:GROUP])
    return jnp.concatenate(parts, axis=0)


def hits(a, b):
    return (a == b).astype(jnp.float32).astype(jnp.bfloat16)


def cell_column(cell):
    rows = jnp.broadcast_to(cell.astype(jnp.float32), (8, ELEMS))
    return jnp.transpose(rows)[:, 0:1].astype(jnp.int32)


def border_cells(kind, index):
    if kind == "circ_low":
        return index
    if kind == "circ_high":
        return index + (EL_C - 1) * STRIP
    if kind == "radial_low":
        return (index // EL_A) * STRIP + index % EL_A
    if kind == "radial_high":
        return (index // EL_A) * STRIP + index % EL_A + (EL_R - 1) * EL_A
    return index * EL_A


def lanes_of(parts, width, rows):
    lane = lax.broadcasted_iota(jnp.int32, (rows, 128), 1) // width
    packed = parts[0:rows]
    for j in range(1, 128 // width):
        packed = jnp.where(lane == j, parts[j * rows : (j + 1) * rows], packed)
    return packed


def rows_of(packed, width, rows):
    lane = lax.broadcasted_iota(jnp.int32, (rows, 128), 1) // width
    return jnp.concatenate(
        [jnp.where(lane == j, packed, 0.0) for j in range(128 // width)], axis=0
    )


def start_all(pairs, sems):
    copies = [pltpu.make_async_copy(src, dst, sems.at[k]) for k, (src, dst) in enumerate(pairs)]
    for copy in copies:
        copy.start()
    return copies


def pack_kernel(
    current,
    cell_ref,
    metric,
    picker_hbm,
    operators_hbm,
    inter,
    circ_low,
    circ_high,
    radial_low,
    radial_high,
    pieces,
    traces,
    operators,
    cells,
    metrics,
    fields,
    picker,
    sems,
):
    side = lax.axis_index("side")
    copies = start_all(
        [(cell_ref, cells), (metric, metrics), (picker_hbm, picker)]
        + [(current.at[f], fields.at[f]) for f in range(FIELDS)]
        + [(operators_hbm, operators)],
        sems,
    )
    iota = lax.broadcasted_iota
    copies[0].wait()
    column = jnp.broadcast_to(cell_column(cells[...]), (ELEMS, 128))
    line = iota(jnp.int32, (1, 128), 1)
    jobs = (
        (circ_low, "circ_low", 0, FACE, 32, CIRC_ROWS),
        (circ_high, "circ_high", FACE, FACE, 32, CIRC_ROWS),
        (radial_low, "radial_low", face_start(1, 0), IFACE, 64, RADIAL_ROWS),
        (radial_high, "radial_high", face_start(1, 1), IFACE, 64, RADIAL_ROWS),
        (inter, "inter", face_start(2, 0), IFACE, 32, INTER_ROWS),
    )
    tables = []
    for out, kind, start, count, width, block in jobs:
        wanted = border_cells(kind, line % width)
        if kind == "inter":
            wanted = wanted + (EL_A - 1) * (1 - side)
        tables.append(hits(column, wanted))
    copies[1].wait()
    copies[2].wait()
    filler = jnp.zeros((FACE - 36, ELEMS), jnp.float32)
    for f in range(FIELDS):
        copies[3 + f].wait()
        traces[f, :FACE] = jnp.concatenate([fields[f, :36], filler], axis=0)
        traces[f, FACE : 2 * FACE] = jnp.concatenate([fields[f, 180:], filler], axis=0)
        for g in range(GROUPS):
            values = fields[f, g * GROUP : (g + 1) * GROUP]
            high = values.astype(jnp.bfloat16).astype(jnp.float32)
            both = jnp.concatenate([high, values - high], axis=0).astype(jnp.bfloat16)
            pieces[f, g] = both
            ends = mm(picker[...], both)
            for k in range(4):
                start = 2 * FACE + k * IFACE + 16 * g
                traces[f, start : start + 16] = ends[16 * k : 16 * k + 16]

    def rows(start, count, total):
        if start == face_start(2, 0):
            parts = [
                jnp.where(side == 0, traces[f, start + count :], traces[f, start : start + count])
                for f in range(FIELDS)
            ]
        else:
            parts = [traces[f, start : start + count] for f in range(FIELDS)]
        extra = total - FIELDS * count
        if extra:
            parts.append(jnp.zeros((extra, ELEMS), jnp.float32))
        return jnp.concatenate(parts, axis=0)

    packed = []
    for table, (out, kind, start, count, width, block) in zip(tables, jobs):
        values = mm_split(rows(start, count, block * (128 // width)), table)
        packed.append(lanes_of(values, width, block))
    even = lax.axis_index("radial") % 2 == 0
    circ_low[...] = packed[0]
    circ_high[...] = packed[1]
    radial_low[...] = jnp.where(even, packed[2], packed[3])
    radial_high[...] = jnp.where(even, packed[3], packed[2])
    inter[...] = packed[4]
    copies[-1].wait()


def jump_terms(exterior, direction, sign, scale):
    first = (WAVE[direction] - sign * FLOW[direction]) * scale
    second = sign * scale
    terms = [first * e for e in exterior]
    terms[0] = terms[0] - second * exterior[1 + direction]
    terms[1 + direction] = terms[1 + direction] - second * exterior[0]
    return terms


def volume_kernel(
    pieces,
    traces,
    operators,
    cells,
    metrics,
    waves_hbm,
    base,
    near_hbm,
    result,
    near,
    waves,
    bases,
    sems,
):
    copies = start_all(
        [(waves_hbm, waves)]
        + [(base.at[f], bases.at[f]) for f in range(FIELDS)]
        + [(near_hbm, near)],
        sems,
    )
    scale = [metrics[d] * WEIGHT for d in range(3)]
    cell = cells[...]
    cell_rows = jnp.broadcast_to(cell_column(cell), (ELEMS, ELEMS))
    place = (cell // STRIP, cell // EL_A % EL_R, cell % EL_A)
    length = (EL_C, EL_R, EL_A)
    stride = (STRIP, EL_A, 1)
    terms = [[] for _ in range(FIELDS)]
    for d in range(3):
        for end in range(2):
            if end == 0:
                wanted = jnp.where(place[d] == 0, -1, cell - stride[d])
            else:
                wanted = jnp.where(place[d] == length[d] - 1, -1, cell + stride[d])
            table = hits(cell_rows, wanted)
            count = face_rows(d)
            start = face_start(d, 1 - end)
            trace = [traces[f, start : start + count] for f in range(FIELDS)]
            outer = mm_split(jnp.concatenate(trace, axis=0), table)
            outer = [outer[f * count : (f + 1) * count] for f in range(FIELDS)]
            found = jump_terms(outer, d, 2.0 * end - 1.0, LIFT * scale[d])
            for f in range(FIELDS):
                terms[f].append(found[f])
    copies[0].wait()
    scaled = jnp.concatenate(scale, axis=0)
    filler = jnp.zeros((5, ELEMS), jnp.float32)
    scale_high = scaled.astype(jnp.bfloat16).astype(jnp.float32)
    scale_rows = jnp.concatenate([scaled, filler, scaled - scale_high, filler], axis=0)
    diagonal = 0.25 + mm(waves[...], scale_rows.astype(jnp.bfloat16))
    own = []
    for f in range(FIELDS):
        products = []
        field = []
        rights = []
        blank = jnp.zeros((ELEMS - 3 * GROUP, ELEMS), jnp.bfloat16)
        for g in range(GROUPS):
            both = pieces[f, g]
            right = jnp.concatenate([both, both[:GROUP], blank], axis=0)
            rights.append(right)
            both = both.astype(jnp.float32)
            field.append(both[:GROUP] + both[GROUP:])
        zero = jnp.zeros((SLAB, ELEMS - 3 * GROUP), jnp.bfloat16)
        left = [jnp.concatenate([operators[g * SLAB : (g + 1) * SLAB], zero], axis=1) for g in range(GROUPS)]
        rates = [mm(jnp.concatenate(left, axis=1), jnp.concatenate(rights, axis=0))[:NODES]]
        zero = jnp.zeros((BLOCK, ELEMS - 3 * GROUP), jnp.bfloat16)
        products = [mm(jnp.concatenate([operators[GROUPS * SLAB : LIFTS], zero], axis=1), r) for r in rights]
        for start in (0, GROUP):
            rates.append(jnp.concatenate([p[start : start + GROUP] for p in products], axis=0))
        total = diagonal * jnp.concatenate(field, axis=0) + lift(operators, terms[f])
        for d in range(3):
            total = total + (FLOW[d] * scale[d]) * rates[d]
        if f == 0:
            pressure = rates
        elif f < 4:
            total = total + scale[f - 1] * pressure[f - 1]
            own[0] = own[0] + scale[f - 1] * rates[f - 1]
        own.append(total)
    for f in range(FIELDS):
        copies[1 + f].wait()
        result[f] = own[f] + 0.75 * bases[f]
    copies[-1].wait()


def border_kernel(
    rotation,
    mortar,
    partial,
    operators,
    near,
    far,
    from_low,
    from_high,
    from_below,
    from_above,
    metrics,
    cells,
    coefficients,
    out,
    result,
    out_sems,
):
    side = lax.axis_index("side")
    radial = lax.axis_index("radial")
    even = radial % 2 == 0
    below = jnp.where(even, from_above[...], from_below[...])
    above = jnp.where(even, from_below[...], from_above[...])
    cell = cells[...]
    scale = [metrics[d] * (WEIGHT * LIFT) for d in range(3)]
    row = lax.broadcasted_iota(jnp.int32, (ELEMS, ELEMS), 0)
    row_of = {32: row % 32, 64: row % 64}
    circ_place = cell // STRIP
    radial_place = cell // EL_A % EL_R
    circ_index = cell % STRIP
    radial_index = circ_place * EL_A + cell % EL_A
    jobs = (
        (from_low[...], jnp.where(circ_place == 0, circ_index, -1), 0, 0, 32, CIRC_ROWS),
        (from_high[...], jnp.where(circ_place == EL_C - 1, circ_index, -1), 0, 1, 32, CIRC_ROWS),
        (below, jnp.where(radial_place == 0, radial_index, -1), 1, 0, 64, RADIAL_ROWS),
        (above, jnp.where(radial_place == EL_R - 1, radial_index, -1), 1, 1, 64, RADIAL_ROWS),
    )
    tables = [hits(row_of[width], index) for _, index, _, _, width, _ in jobs]
    remainder = rotation[0] % EL_C
    first = jnp.where(side == 0, remainder, EL_C - 1 - remainder)
    facing = cell % EL_A == (EL_A - 1) * (1 - side)
    pickers = []
    for later in range(2):
        at = circ_place + first + later
        index = at * EL_R + radial_place
        early_index = jnp.where(facing & (at < EL_C), index, -1)
        late_index = jnp.where(facing & (at >= EL_C), index - EL_C * EL_R, -1)
        pickers.append((hits(row_of[32], early_index), hits(row_of[32], late_index)))
    fraction = jnp.zeros_like(cell)
    for r in range(EL_R):
        fraction = jnp.where(radial_place == r, mortar[r], fraction)
    chosen = lax.broadcasted_iota(jnp.int32, (48, ELEMS), 0) % 16 == fraction + 8 * side
    weights = mm(coefficients[...], chosen.astype(jnp.float32).astype(jnp.bfloat16))

    def both(values):
        high = values.astype(jnp.bfloat16).astype(jnp.float32)
        return jnp.concatenate([high, values - high], axis=1).astype(jnp.bfloat16)

    terms = [[] for _ in range(FIELDS)]
    for table, (source, _, d, end, width, block) in zip(tables, jobs):
        outer = mm(both(rows_of(source, width, block)), table)
        count = face_rows(d)
        outer = [outer[f * count : (f + 1) * count] for f in range(FIELDS)]
        factor = scale[d]
        if d == 1:
            wall = 0 if end == 0 else 3
            factor = factor * jnp.where(radial == wall, 0.0, 1.0)
        found = jump_terms(outer, d, 2.0 * end - 1.0, factor)
        for f in range(FIELDS):
            terms[f].append(found[f])
    earlier = jnp.where(side == 0, near[...], far[...])
    later = jnp.where(side == 0, far[...], near[...])
    earlier_parts = both(rows_of(earlier, 32, INTER_ROWS))
    later_parts = both(rows_of(later, 32, INTER_ROWS))
    windows = [mm(earlier_parts, a) + mm(later_parts, b) for a, b in pickers]
    outer = []
    for f in range(FIELDS):
        blocks = []
        for i in range(6):
            total = None
            for later in range(2):
                for j in range(6):
                    at = 40 * later + 6 * i + j
                    start = f * IFACE + 8 * j
                    part = weights[at : at + 1] * windows[later][start : start + 8]
                    total = part if total is None else total + part
            blocks.append(total)
        outer.append(jnp.concatenate(blocks, axis=0))
    sign = jnp.where(side == 0, 1.0, -1.0)
    found = jump_terms(outer, 2, sign, scale[2])
    stores = []
    for f in range(FIELDS):
        terms[f].append(jnp.where(side == 1, found[f], 0.0))
        terms[f].append(jnp.where(side == 0, found[f], 0.0))
        result[f] = partial[f] + lift(operators, terms[f])
        stores.append(pltpu.make_async_copy(result.at[f], out.at[f], out_sems.at[f]))
        stores[f].start()
    for store in stores:
        store.wait()


def to_partner(shift):
    def send(block):
        pairs = []
        for k in range(32):
            other = (k + shift) % 32
            pairs += [(2 * k, 2 * other + 1), (2 * other + 1, 2 * k)]
        return lax.ppermute(block, ("circ", "side"), pairs)

    return send


def to_beside(block):
    pairs = []
    for k in range(32):
        pairs += [(2 * k, 2 * ((k - 1) % 32)), (2 * k + 1, 2 * ((k + 1) % 32) + 1)]
    return lax.ppermute(block, ("circ", "side"), pairs)


def ring(block, axis, step):
    count = lax.axis_size(axis)
    return lax.ppermute(block, axis, [(i, (i + step) % count) for i in range(count)])


def swap(block, first):
    count = lax.axis_size("radial")
    step = 1 if first else -1
    pairs = [(i, (i + (step if i % 2 == 0 else -step)) % count) for i in range(count)]
    return lax.ppermute(block, "radial", pairs)


def constant(values):
    return jnp.asarray(np.asarray(values), dtype=jnp.bfloat16)


def local(current, section_base, metric, slot_cell, rotation, mortar_index):
    current = current.reshape(FIELDS, NODES, ELEMS)
    section_base = section_base.reshape(FIELDS, NODES, ELEMS)
    metric = metric.reshape(3, 1, ELEMS)
    cell = slot_cell.reshape(1, ELEMS)
    params = pltpu.CompilerParams(vmem_limit_bytes=24 * 1024 * 1024)
    smem = pl.BlockSpec(memory_space=pltpu.SMEM)
    vmem = pl.BlockSpec(memory_space=pltpu.VMEM)
    anywhere = pl.BlockSpec(memory_space=pl.ANY)
    whole = (FIELDS, NODES, ELEMS)

    def buffer(*dims, kind=jnp.float32):
        return pltpu.VMEM(dims, kind)

    current, section_base, metric, cell = (
        pltpu.with_memory_space_constraint(x, pltpu.HBM)
        for x in (current, section_base, metric, cell)
    )
    tables = node_tables()
    picker = group_picker()
    packed = pl.pallas_call(
        pack_kernel,
        in_specs=[anywhere] * 5,
        out_specs=[vmem] * 10,
        out_shape=[
            buffer(INTER_ROWS, 128),
            buffer(CIRC_ROWS, 128),
            buffer(CIRC_ROWS, 128),
            buffer(RADIAL_ROWS, 128),
            buffer(RADIAL_ROWS, 128),
            buffer(FIELDS, GROUPS, 2 * GROUP, ELEMS, kind=jnp.bfloat16),
            buffer(FIELDS, FACES, ELEMS),
            buffer(*tables.shape, kind=jnp.bfloat16),
            buffer(1, ELEMS, kind=jnp.int32),
            buffer(3, 1, ELEMS),
        ],
        scratch_shapes=[
            buffer(*whole),
            buffer(*picker.shape, kind=jnp.bfloat16),
            pltpu.SemaphoreType.DMA((4 + FIELDS,)),
        ],
        compiler_params=params,
        name="pack",
    )(
        current,
        cell,
        metric,
        pltpu.with_memory_space_constraint(constant(picker), pltpu.HBM),
        pltpu.with_memory_space_constraint(constant(tables), pltpu.HBM),
    )
    inter, circ_low, circ_high, radial_low, radial_high = packed[:5]
    pieces, traces, operators, cells, metrics = packed[5:]
    from_low = ring(circ_high, "circ", 1)
    from_high = ring(circ_low, "circ", -1)
    from_below = swap(radial_high, True)
    from_above = swap(radial_low, False)
    near = lax.switch(
        jnp.right_shift(rotation[0], 3), [to_partner(k) for k in range(32)], inter
    )
    far = to_beside(near)
    metrics, near = lax.optimization_barrier((metrics, near))
    partial, near = pl.pallas_call(
        volume_kernel,
        in_specs=[vmem] * 5 + [anywhere] * 3,
        out_specs=[vmem] * 2,
        out_shape=[buffer(*whole), buffer(INTER_ROWS, 128)],
        scratch_shapes=[
            buffer(NODES, 16, kind=jnp.bfloat16),
            buffer(*whole),
            pltpu.SemaphoreType.DMA((2 + FIELDS,)),
        ],
        compiler_params=params,
        cost_estimate=pl.CostEstimate(
            flops=4 * 10**9, bytes_accessed=4 * 10**6, transcendentals=0
        ),
        name="volume",
    )(
        pieces,
        traces,
        operators,
        cells,
        metrics,
        pltpu.with_memory_space_constraint(constant(wave_columns()), pltpu.HBM),
        section_base,
        near,
    )
    out = pl.pallas_call(
        border_kernel,
        in_specs=[smem, smem] + [vmem] * 11,
        out_specs=anywhere,
        out_shape=jax.ShapeDtypeStruct(whole, jnp.float32),
        scratch_shapes=[buffer(*whole), pltpu.SemaphoreType.DMA((FIELDS,))],
        compiler_params=params,
        name="border",
    )(
        rotation,
        mortar_index,
        partial,
        operators,
        near,
        far,
        from_low,
        from_high,
        from_below,
        from_above,
        metrics,
        cells,
        constant(mortar_columns()),
    )
    return out.reshape(1, 1, 1, FIELDS, NODES, ELEMS)


def solution(mesh):
    return jax.shard_map(
        local,
        mesh=mesh,
        in_specs=(
            P("side", "circ", "radial", None, None, None),
            P("side", "circ", "radial", None, None, None),
            P("side", "circ", "radial", None, None),
            P("side", "circ", "radial", None),
            P(),
            P("radial"),
        ),
        out_specs=P("side", "circ", "radial", None, None, None),
        check_vma=False,
    )
```
